512 devices in a mesh: expert: 16 (over z), tensor: 32 (over y, x, core).
Axes of the slice: x: 4, y: 4, z: 16, core: 2. Of those that a mesh axis runs over, the one named last changes fastest.
Arguments:
- tokens: bfloat16 [1024, 3072], P('expert', 'tensor'), may hold values from -6 to 6
- grad_out: bfloat16 [1024, 3072], P('expert', 'tensor'), may hold values from -3 to 3
- probs: bfloat16 [1024, 4], P('expert'), may hold values from 0.049804688 to 0.5
- routes: int32 [1024, 4], P('expert'), may hold values from 0 to 15, all different within a row; in each aligned block of 64 rows (0 to 63, 64 to 127, ...) at most 20 rows name the same one
- gate_weight: bfloat16 [16, 5376, 3072], P('expert', 'tensor'), may hold values from -0.109375 to 0.109375
- up_weight: bfloat16 [16, 5376, 3072], P('expert', 'tensor'), may hold values from -0.109375 to 0.109375
- down_weight: bfloat16 [16, 5376, 3072], P('expert', 'tensor'), may hold values from -0.078125 to 0.078125
Outputs:
- d_tokens: bfloat16 [1024, 3072], P('expert', 'tensor')
- d_probs: float32 [1024, 4], P('expert')
- d_down: bfloat16 [16, 5376, 3072], P('expert', 'tensor')
The draws below stay inside these ranges and needn't reach their ends.
Inputs may be any that keep to these rules, and one draw needn't show every extreme that they name: Each token's 4 experts differ. Among the 64 tokens of one index of expert, no expert is named by more than 20 routes, a bound that some block reaches of them.
All inputs are finite; a program needn't handle non-finite values.
Results may differ from the reference program's by a relative error of at most 0.007.
Values may be sent and summed in bfloat16 or wider, within the bound.
No kernel may reach another device: no remote copies, remote signals or barrier semaphores. Data moves between devices by JAX's collectives and lax.ppermute only.
A program may use at most 128 MiB of HBM per device.

```python
import math
import jax
import jax.numpy as jnp
import numpy as np
from jax import lax

D = 3072
FF = 5376
TOP = 4
TOK_DEV = 64
EXPERTS = 16
CAP = 20
TOKENS = 1024
N_EXPERT = 16


def level_of(own_key, extent, cuts, least, largest):
    def one(dim, shards_of):
        draws = jax.random.uniform(jax.random.fold_in(jax.random.fold_in(own_key, 6), dim), (shards_of,), jnp.float32, least / len(cuts), largest / len(cuts))
        return jnp.repeat(jnp.exp(draws), extent[dim] // shards_of).reshape((-1,) + (1,) * (len(extent) - dim - 1))

    factor_of = one(*cuts[0])
    for cut in cuts[1:]:
        factor_of = factor_of * one(*cut)
    return factor_of


def assign_block(rng, own, number, rows, amount, top, reach, slope):
    ranking = jax.random.permutation(rng, amount)
    crowded, common = shares(amount, rows * top, reach, slope, True), shares(amount, rows * top, reach, slope, False)
    places = jnp.arange(amount)

    def named(sizes, turn):
        used = int((sizes > 0).sum())
        fixed = max(1, used // 4)
        moved = fixed + (places - fixed + turn * (used - fixed)) % max(1, amount - fixed)
        return jnp.zeros((amount,), jnp.int32).at[ranking[jnp.where(places < fixed, places, moved)]].set(jnp.asarray(sizes, jnp.int32))

    sizes = jnp.where(number % 4 == 0, named(crowded, number // 4), named(common, number - number // 4 - 1))
    mixed = jax.random.permutation(jax.random.fold_in(own, 3), amount)
    giver, sink = mixed[0:amount // 2 * 2:2], mixed[1:amount // 2 * 2:2]
    slack = jnp.minimum(sizes[giver] - 1, reach - sizes[sink]) // 2
    slack = jnp.where((giver == ranking[0]) | (sink == ranking[0]) | (sizes[sink] == 0), 0, jnp.maximum(slack, 0))
    moved = jax.random.randint(jax.random.fold_in(own, 4), (amount // 2,), 0, 1 << 20) % (slack + 1)
    sizes = sizes.at[giver].add(-moved).at[sink].add(moved)
    labels = jnp.searchsorted(jnp.cumsum(sizes), jnp.arange(rows * top), side="right").astype(jnp.int32)
    table = labels.reshape(top, rows).T
    table = table[jax.random.permutation(jax.random.fold_in(own, 1), rows)]
    turn = jax.random.randint(jax.random.fold_in(own, 2), (rows, 1), 0, top)
    return jnp.take_along_axis(table, (jnp.arange(top)[None, :] + turn) % top, axis=1)


def shares(amount, total, reach, skew, full):
    loads = [(1 << 20) // math.isqrt(rank ** skew) + 1 for rank in range(1, amount + 1)]
    largest = reach if full else min(reach, max(-(-total // amount), total * loads[0] // sum(loads)))
    least = 1 if total - largest >= amount - 1 else 0
    given, surplus = [largest] + [least] * (amount - 1), total - largest - least * (amount - 1)
    while surplus > 0:
        candidates = [i for i in range(1, amount) if given[i] < largest] or [i for i in range(1, amount) if given[i] < reach]
        mass, left = sum([loads[i] for i in candidates]), surplus
        for i in candidates:
            addition = min(reach - given[i], max(1, left * loads[i] // mass), surplus)
            given[i] = given[i] + addition
            surplus = surplus - addition
    return np.array(given)


def bell_draw(rng, dims, deviation, most, shards=(), kind=jnp.bfloat16):
    level = level_of(rng, dims, shards, -0.22, 0.18) if shards else 1.0
    entries = jax.random.normal(rng, dims, jnp.float32) * deviation * level
    return jnp.minimum(jnp.maximum(entries, -most), most).astype(kind)


def setup_inputs(seed: int = 0) -> dict:
    streams_of = jax.random.split(jax.random.key(seed), 8)
    tokens = bell_draw(streams_of[0], (TOKENS, D), 1.0, 6.0, ((0, 16), (1, 32)))
    grad_out = bell_draw(streams_of[1], (TOKENS, D), 0.5, 3.0, ((0, 16), (1, 32)))
    probs = jnp.clip(jnp.exp(math.log(0.5) - 2.306499 * jax.random.uniform(streams_of[2], (TOKENS, TOP), jnp.float32) ** level_of(streams_of[2], (TOKENS, TOP), ((0, 16),), -0.2, 0.2)), 0.049804688, 0.5).astype(jnp.bfloat16)
    routes_keys = jax.random.split(jax.random.fold_in(streams_of[3], 1), TOKENS // TOK_DEV)
    routes_turns = jax.random.permutation(jax.random.fold_in(streams_of[3], 3), TOKENS // TOK_DEV)
    routes = jax.vmap(lambda own, number: assign_block(jax.random.fold_in(streams_of[3], 2), own, number, TOK_DEV, EXPERTS, TOP, CAP, 2))(routes_keys, routes_turns).reshape((TOKENS, TOP))
    gate_weight = bell_draw(streams_of[4], (EXPERTS, FF, D), D ** -0.5, 0.109375, ((0, 16), (1, 32)))
    up_weight = bell_draw(streams_of[5], (EXPERTS, FF, D), D ** -0.5, 0.109375, ((0, 16), (1, 32)))
    down_weight = bell_draw(streams_of[6], (EXPERTS, FF, D), FF ** -0.5, 0.078125, ((0, 16), (1, 32)))
    return dict(tokens=tokens, grad_out=grad_out, probs=probs, routes=routes, gate_weight=gate_weight, up_weight=up_weight, down_weight=down_weight)


def block_positions(flat_routes):
    experts_iota = jnp.arange(EXPERTS, dtype=jnp.int32)
    onehot = (flat_routes[:, None] == experts_iota[None, :]).astype(jnp.int32)
    before = jnp.cumsum(onehot, axis=0) - onehot
    return jnp.sum(before * onehot, axis=1).astype(jnp.int32)


def reference(tokens, grad_out, probs, routes, gate_weight, up_weight, down_weight):
    blocks = routes.reshape(N_EXPERT, TOK_DEV * TOP)
    position = jax.vmap(block_positions)(blocks)
    source = jnp.arange(N_EXPERT, dtype=jnp.int32)[:, None]
    row_index = (source * CAP + position).reshape(-1).astype(jnp.int32)
    expert_of = routes.reshape(-1).astype(jnp.int32)
    pair_ids = jnp.arange(TOKENS * TOP, dtype=jnp.int32)
    pair_table = jnp.full((EXPERTS, N_EXPERT * CAP), -1, dtype=jnp.int32)
    pair_table = pair_table.at[expert_of, row_index].set(pair_ids)
    flat_probs = probs.reshape(-1)

    def expert_grads(packed):
        pairs, w_gate, w_up, w_down = packed
        valid = pairs >= 0
        safe = jnp.where(valid, pairs, 0).astype(jnp.int32)
        token_ids = (safe // TOP).astype(jnp.int32)
        rows_x = jnp.where(valid[:, None], tokens[token_ids], 0).astype(jnp.bfloat16)
        rows_dy = jnp.where(valid[:, None], grad_out[token_ids], 0).astype(jnp.bfloat16)
        prob_rows = jnp.where(valid, flat_probs[safe].astype(jnp.float32), 0.0).astype(jnp.float32)
        pre_gate = jnp.dot(rows_x, w_gate.T, preferred_element_type=jnp.float32)
        pre_up = jnp.dot(rows_x, w_up.T, preferred_element_type=jnp.float32)
        sigmoid_a = jax.nn.sigmoid(pre_gate)
        silu_a = pre_gate * sigmoid_a
        hidden = (silu_a * pre_up).astype(jnp.bfloat16)
        back_hidden = jnp.dot(rows_dy, w_down.T, preferred_element_type=jnp.float32)
        scores = jnp.sum(hidden.astype(jnp.float32) * back_hidden, axis=1)
        scaled_hidden = (prob_rows[:, None] * hidden.astype(jnp.float32)).astype(jnp.bfloat16)
        down_grad = jnp.dot(scaled_hidden.T, rows_dy, preferred_element_type=jnp.float32).astype(jnp.bfloat16)
        hidden_grad = prob_rows[:, None] * back_hidden
        grad_gate = (hidden_grad * pre_up * sigmoid_a * (1.0 + pre_gate * (1.0 - sigmoid_a))).astype(jnp.bfloat16)
        grad_up = (hidden_grad * silu_a).astype(jnp.bfloat16)
        input_grad = jnp.dot(grad_gate, w_gate, preferred_element_type=jnp.float32) + jnp.dot(grad_up, w_up, preferred_element_type=jnp.float32)
        return input_grad, scores, down_grad

    input_grads, all_scores, d_down = lax.map(expert_grads, (pair_table, gate_weight, up_weight, down_weight))
    pairs_all = pair_table.reshape(-1)
    valid_all = pairs_all >= 0
    safe_all = jnp.where(valid_all, pairs_all, 0).astype(jnp.int32)
    token_all = (safe_all // TOP).astype(jnp.int32)
    grads_flat = jnp.where(valid_all[:, None], input_grads.reshape(-1, D), 0.0).astype(jnp.float32)
    d_tokens = jnp.zeros((TOKENS, D), jnp.float32).at[token_all].add(grads_flat).astype(jnp.bfloat16)
    scores_flat = jnp.where(valid_all, all_scores.reshape(-1), 0.0).astype(jnp.float32)
    d_probs = jnp.zeros((TOKENS * TOP,), jnp.float32).at[safe_all].add(scores_flat).reshape(TOKENS, TOP)
    return d_tokens, d_probs, d_down
```

```python
import jax
import jax.numpy as jnp
from jax import lax
from jax.experimental import pallas as pl
from jax.experimental.pallas import tpu as pltpu
from jax.sharding import PartitionSpec as P

F32 = jnp.float32
BF16 = jnp.bfloat16
I32 = jnp.int32

EXPERTS = 16
CHIPS = 16
CAP = 20
SLOTS = EXPERTS * CAP
WIDE = 384
TOK = 64
TOP = 4
FEAT = 96
HID = 168
D = 3072
BLOCK = 32


def iota(shape, dim):
    return lax.broadcasted_iota(I32, shape, dim)


def flag(condition):
    return jnp.where(condition, 1.0, 0.0).astype(F32)


def hot(condition):
    return flag(condition).astype(BF16)


def dot(a, b):
    return jnp.dot(a, b, preferred_element_type=F32)


def dot_first(a, b):
    return lax.dot_general(a, b, (((0,), (0,)), ((), ())), preferred_element_type=F32)


def dot_last(a, b):
    return lax.dot_general(a, b, (((1,), (1,)), ((), ())), preferred_element_type=F32)


def expert_of(slot):
    return lax.shift_right_logical(slot * 3277, 16)


def params(mib, **kw):
    return pltpu.CompilerParams(vmem_limit_bytes=mib * 1024 * 1024, **kw)


def cost(flops):
    return pl.CostEstimate(flops=int(flops), bytes_accessed=4 << 20, transcendentals=0)


def pack_kernel(routes_hbm, probs_hbm, x_hbm, dy_hbm, out_ref, row_ref, routes_ref, probs_ref, x_ref, dy_ref, sems):
    pairs = ((routes_hbm, routes_ref), (probs_hbm, probs_ref), (x_hbm, x_ref), (dy_hbm, dy_ref))
    loads = [pltpu.make_async_copy(src, dst, sems.at[i]) for i, (src, dst) in enumerate(pairs)]
    for load in loads:
        load.start()
    for load in loads:
        load.wait()
    routes = routes_ref[...]
    probs = probs_ref[...].astype(F32)
    experts = iota((EXPERTS, TOK), 0)
    hits = [routes[k : k + 1, :] == experts for k in range(TOP)]
    member = sum(flag(h) for h in hits)
    weight = sum(jnp.where(hits[k], probs[k : k + 1, :], 0.0) for k in range(TOP))
    upper = hot(iota((TOK, TOK), 0) < iota((TOK, TOK), 1))
    count = dot(member.astype(BF16), upper)
    place = jnp.where(member > 0.5, count, -1.0)
    target = count + (experts * BLOCK).astype(F32)
    rows_of = [jnp.sum(jnp.where(hits[k], target, 0.0), axis=0, keepdims=True) for k in range(TOP)]
    kth = iota((8, TOK), 0)
    row_ref[...] = sum(jnp.where(kth == k, rows_of[k], 0.0) for k in range(TOP)).astype(I32)

    rows = EXPERTS * BLOCK
    expand = hot(lax.shift_right_logical(iota((rows, EXPERTS), 0), 5) == iota((rows, EXPERTS), 1))
    place_rows = dot(expand, place.astype(BF16))
    weight_rows = dot(expand, weight.astype(BF16))
    s_int = iota((rows, TOK), 0) & (BLOCK - 1)
    s = s_int.astype(F32)
    tail = (s_int >= CAP) & (s_int < 30)
    main = flag((place_rows == s) & (s_int < CAP))
    left = hot((place_rows == s - 20.0) & tail)
    right = hot((place_rows == s - 10.0) & tail)

    x = x_ref[...]
    dy = dy_ref[...]
    f = iota((FEAT, 128), 0)
    lane = iota((FEAT, 128), 1)
    b_main = dot(x, hot(lane == f)) + dot(dy, hot((lane == f + 96) & (f < 32)))
    b_left = dot(dy, hot((lane == f - 32) & (f >= 32)))
    b_right = dot(dy, hot((lane == f + 32) & (f >= 32)))

    prob_col = jnp.sum(main * weight_rows, axis=1, keepdims=True)
    s_lane = iota((rows, 128), 0) & (BLOCK - 1)
    prob_wide = jnp.where(s_lane == iota((rows, 128), 1), prob_col, 0.0).astype(BF16)
    gather = hot(lax.shift_right_logical(iota((EXPERTS, rows), 1), 5) == iota((EXPERTS, rows), 0))
    prob_block = dot(gather, prob_wide).astype(BF16)
    at_30 = hot(iota((rows, EXPERTS), 0) == iota((rows, EXPERTS), 1) * BLOCK + 30)

    out = (
        dot(main.astype(BF16), b_main.astype(BF16))
        + dot(left, b_left.astype(BF16))
        + dot(right, b_right.astype(BF16))
        + dot(at_30, prob_block)
    )
    out_ref[...] = out.astype(BF16).reshape(EXPERTS, BLOCK, 128)


def spread_kernel(got_ref, out_ref, prob_ref):
    rows = EXPERTS * BLOCK
    got = got_ref[...].reshape(rows, 128)
    n = iota((1, WIDE), 1)
    e_x = expert_of(n)
    s_x = n - e_x * CAP
    to_x = jnp.where(n < SLOTS, e_x * BLOCK + s_x, -1)
    slot = jnp.where(n < 128, n + 192, n - 128)
    e_d = expert_of(slot)
    s_d = slot - e_d * CAP
    live = n >= 64
    to_d = jnp.where(live, e_d * BLOCK + s_d, -1)
    to_left = jnp.where(live & (s_d < 10), e_d * BLOCK + 20 + s_d, -1)
    to_right = jnp.where(live & (s_d >= 10), e_d * BLOCK + 10 + s_d, -1)
    r = iota((rows, WIDE), 0)
    part_x = dot_first(got, hot(r == to_x))
    part_d = dot_first(got, hot(r == to_d))
    part_l = dot_first(got, hot(r == to_left))
    part_r = dot_first(got, hot(r == to_right))
    x_t = part_x[0:FEAT]
    d_t = jnp.concatenate([part_d[96:128], part_l[0:64] + part_r[64:128]], axis=0)
    first = x_t[:, 0:256].astype(BF16)
    middle = (x_t[:, 256:384] + d_t[:, 0:128]).astype(BF16)
    last = d_t[:, 128:384].astype(BF16)
    for j in range(CHIPS):
        out_ref[j, :, 0:256] = first
        out_ref[j, :, 256:384] = middle
        out_ref[j, :, 384:640] = last

    pick = hot(iota((EXPERTS, rows), 1) == iota((EXPERTS, rows), 0) * BLOCK + 30)
    per_expert = dot(pick, got).astype(BF16)
    wide = dot(per_expert, hot(iota((128, WIDE), 0) == s_x))
    probs = jnp.sum(jnp.where(iota((EXPERTS, WIDE), 0) == e_x, wide, 0.0), axis=0, keepdims=True)
    prob_ref[...] = jnp.broadcast_to(probs, (8, WIDE))


def score_rows(scores):
    row = iota((16, 128), 0)
    return (
        jnp.where(row == 0, scores[:, 0:128], 0.0)
        + jnp.where(row == 1, scores[:, 128:256], 0.0)
        + jnp.where(row == 2, scores[:, 256:384], 0.0)
    )


def split_rows(scores):
    high = scores.astype(BF16).astype(F32)
    low = (scores - high).astype(BF16).astype(F32)
    return (high + pltpu.roll(low, 3, 0)).astype(BF16)


def squeeze(piece):
    last = piece[:, 256:384]
    lane = iota((48, 128), 1)
    both = jnp.where(lane < 64, last[0:48], pltpu.roll(last[48:96], 64, 1))
    return piece[:, 0:128], piece[:, 128:256], both


def this_core():
    return lax.rem(lax.axis_index("tensor"), 2)


def turn_kernel(own_ref, gate_ref, up_ref, rows_ref, gate_t_ref, up_t_ref):
    core = this_core()
    first = core == 0
    for j in range(CHIPS):
        rows_ref[j, core] = own_ref[j]
    for weight_ref, turned_ref in ((gate_ref, gate_t_ref), (up_ref, up_t_ref)):
        for i in range(CHIPS // 2):
            turned = weight_ref[0, :, pl.ds(i * 384, 384)].T
            for half in range(2):
                even = turned[192 * half : 192 * half + 96]
                odd = turned[192 * half + 96 : 192 * half + 192]
                turned_ref[0, 2 * i + half] = jnp.where(first, odd, even)
                turned_ref[1, 2 * i + half] = jnp.where(first, even, odd)


def input_grads(turned, gate_t_ref, up_t_ref, grad_gate, grad_up, out_ref):
    for i in range(0, CHIPS, 4):
        part = pl.ds(i, 4)
        sums = dot(gate_t_ref[turned, part].reshape(384, HID), grad_gate)
        sums = sums + dot(up_t_ref[turned, part].reshape(384, HID), grad_up)
        for j in range(4):
            a, b, c = squeeze(sums[96 * j : 96 * j + 96])
            out_ref[i + j, 0:96] = a.astype(out_ref.dtype)
            out_ref[i + j, 96:192] = b.astype(out_ref.dtype)
            out_ref[i + j, 192:240] = c.astype(out_ref.dtype)


def middle_kernel(
    rows_in_ref,
    other_ref,
    gate_ref,
    up_ref,
    down_ref,
    prob_ref,
    gate_t_ref,
    up_t_ref,
    rows_ref,
    send_ref,
    score_ref,
    hid_ref,
):
    del rows_in_ref
    core = this_core()
    for j in range(CHIPS):
        rows_ref[j, 1 - core] = other_ref[j]
    rows = rows_ref[...].reshape(D, 640)
    x_t = rows[:, 0:384]
    dy_t = rows[:, 256:640]
    pre_gate = dot(gate_ref[0], x_t)
    pre_up = dot(up_ref[0], x_t)
    raw = dot(down_ref[0], dy_t)
    back = jnp.concatenate([raw[:, 128:384], pltpu.roll(raw[:, 0:128], 64, 1)], axis=1)
    live = iota((1, WIDE), 1) < SLOTS
    back = jnp.where(live, back, 0.0)
    probs = prob_ref[0:1, :]
    sig = jax.nn.sigmoid(pre_gate)
    silu = pre_gate * sig
    hidden = (silu * pre_up).astype(BF16).astype(F32)
    scores = score_rows(jnp.sum(hidden * back, axis=0, keepdims=True))
    scaled = jnp.where(live, probs * hidden, 0.0)
    back_p = probs * back
    grad_gate = jnp.where(live, back_p * pre_up * sig * (1.0 + pre_gate * (1.0 - sig)), 0.0).astype(BF16)
    grad_up = (back_p * silu).astype(BF16)
    input_grads(0, gate_t_ref, up_t_ref, grad_gate, grad_up, send_ref)
    parts = split_rows(scores)
    for j in range(CHIPS):
        send_ref[j, 240:256] = parts
    score_ref[...] = scores
    scaled = jnp.concatenate([pltpu.roll(scaled[:, 256:384], 64, 1), scaled[:, 0:256]], axis=1)
    hid_ref[0] = scaled.astype(BF16)
    hid_ref[1] = grad_gate
    hid_ref[2] = grad_up


def rest_kernel(rows_ref, hid_ref, gate_t_ref, up_t_ref, keep_ref, d_down_ref):
    d_down_ref[0] = dot_last(hid_ref[0], rows_ref[...].reshape(D, 640)[:, 256:640]).astype(BF16)
    input_grads(1, gate_t_ref, up_t_ref, hid_ref[1], hid_ref[2], keep_ref)


def join_kernel(keep_ref, score_ref, got_ref, out_ref):
    got = got_ref[0, 240:256].astype(F32)
    row = iota((16, 128), 0)
    total = score_ref[...] + got + pltpu.roll(got, 13, 0)
    parts = split_rows(jnp.where(row < 3, total, 0.0))
    for j in range(CHIPS):
        out_ref[j, 0:240] = (keep_ref[j, 0:240] + got_ref[j, 0:240].astype(F32)).astype(BF16)
        out_ref[j, 240:256] = parts


def fold_kernel(got_ref, out_ref):
    total = got_ref[0].astype(F32)
    for j in range(1, CHIPS):
        total = total + got_ref[j].astype(F32)
    both = total[192:240]
    lane = iota((48, 128), 1)
    last = jnp.concatenate(
        [jnp.where(lane < 64, both, 0.0), jnp.where(lane < 64, pltpu.roll(both, 64, 1), 0.0)], axis=0
    )
    grads = jnp.concatenate([total[0:96], total[96:192], last], axis=1)
    tail = total[240:256]
    score = tail + pltpu.roll(tail, 13, 0)
    wide = jnp.concatenate([score[0:1], score[1:2], score[2:3]], axis=1)
    high = wide.astype(BF16).astype(F32)
    low = wide - high
    row = iota((32, WIDE), 0)
    extra = jnp.where(row == 0, high, 0.0) + jnp.where(row == 1, low, 0.0)
    table = jnp.concatenate([grads, extra], axis=0).astype(BF16)
    n = iota((1, WIDE), 1)
    e = expert_of(n)
    to = jnp.where(n < SLOTS, e * BLOCK + (n - e * CAP), -1)
    pick = hot(iota((EXPERTS * BLOCK, WIDE), 0) == to)
    out_ref[...] = dot_last(pick, table).astype(BF16).reshape(EXPERTS, BLOCK, 128)


def combine_kernel(got_ref, row_ref, d_tokens_ref, d_probs_ref):
    rows = EXPERTS * BLOCK
    got = got_ref[...].reshape(rows, 128)
    r = iota((rows, TOK), 0)
    picks = [flag(r == row_ref[k : k + 1, :]) for k in range(TOP)]
    d_tokens_ref[...] = dot_first(sum(picks).astype(BF16), got)[:, 0:FEAT].astype(BF16)
    lane = iota((rows, 128), 1)
    score = jnp.where((lane == 96) | (lane == 97), got.astype(F32), 0.0)
    score = jnp.sum(score, axis=1, keepdims=True)
    for k in range(TOP):
        d_probs_ref[k : k + 1, :] = jnp.sum(picks[k] * score, axis=0, keepdims=True)


def struct(*shape, dtype):
    return jax.ShapeDtypeStruct(shape, dtype)


SAME_CORE = [[2 * j + core for j in range(CHIPS)] for core in range(2)]
OTHER_CORE = [(i, i ^ 1) for i in range(2 * CHIPS)]


def per_device(tokens, grad_out, probs, routes, gate_weight, up_weight, down_weight):
    packed, row_of = pl.pallas_call(
        pack_kernel,
        out_shape=(pltpu.VMEM((EXPERTS, BLOCK, 128), BF16), pltpu.VMEM((8, TOK), I32)),
        in_specs=[pl.BlockSpec(memory_space=pltpu.HBM)] * 4,
        scratch_shapes=[
            pltpu.VMEM((TOP, TOK), I32),
            pltpu.VMEM((TOP, TOK), BF16),
            pltpu.VMEM((TOK, FEAT), BF16),
            pltpu.VMEM((TOK, FEAT), BF16),
            pltpu.SemaphoreType.DMA((4,)),
        ],
        compiler_params=params(60),
        name="pack",
    )(routes.T, probs.T, tokens, grad_out)
    got = lax.all_to_all(packed, "expert", 0, 0, tiled=True)
    copies, prob_rows = pl.pallas_call(
        spread_kernel,
        out_shape=(struct(CHIPS, FEAT, 640, dtype=BF16), struct(8, WIDE, dtype=F32)),
        compiler_params=params(16),
        name="spread",
    )(got)
    own = lax.all_to_all(copies, "tensor", 0, 0, tiled=True, axis_index_groups=SAME_CORE)
    other = lax.ppermute(own, "tensor", OTHER_CORE)
    rows, gate_t, up_t = pl.pallas_call(
        turn_kernel,
        out_shape=(
            struct(CHIPS, 2, FEAT, 640, dtype=BF16),
            struct(2, CHIPS, FEAT, HID, dtype=BF16),
            struct(2, CHIPS, FEAT, HID, dtype=BF16),
        ),
        compiler_params=params(20),
        cost_estimate=cost(8e9),
        name="turn",
    )(own, gate_weight, up_weight)
    rows, send, score, hid = pl.pallas_call(
        middle_kernel,
        out_shape=(
            struct(CHIPS, 2, FEAT, 640, dtype=BF16),
            struct(CHIPS, 256, 128, dtype=BF16),
            struct(16, 128, dtype=F32),
            struct(3, HID, WIDE, dtype=BF16),
        ),
        input_output_aliases={0: 0},
        compiler_params=params(24),
        cost_estimate=cost(4e9),
        name="middle",
    )(rows, other, gate_weight, up_weight, down_weight, prob_rows, gate_t, up_t)
    partner = lax.ppermute(send, "tensor", OTHER_CORE)
    keep, d_down = pl.pallas_call(
        rest_kernel,
        out_shape=(struct(CHIPS, 240, 128, dtype=F32), struct(1, HID, D, dtype=BF16)),
        compiler_params=params(20),
        cost_estimate=cost(4e9),
        name="rest",
    )(rows, hid, gate_t, up_t)
    joined = pl.pallas_call(
        join_kernel,
        out_shape=struct(CHIPS, 256, 128, dtype=BF16),
        compiler_params=params(16),
        name="join",
    )(keep, score, partner)
    shares = lax.all_to_all(joined, "tensor", 0, 0, tiled=True, axis_index_groups=SAME_CORE)
    folded = pl.pallas_call(
        fold_kernel,
        out_shape=struct(EXPERTS, BLOCK, 128, dtype=BF16),
        compiler_params=params(16),
        name="fold",
    )(shares)
    back = lax.all_to_all(folded, "expert", 0, 0, tiled=True)
    d_tokens, d_probs = pl.pallas_call(
        combine_kernel,
        out_shape=(struct(TOK, FEAT, dtype=BF16), struct(TOP, TOK, dtype=F32)),
        compiler_params=params(16),
        name="combine",
    )(back, row_of)
    return d_tokens, d_probs.T, d_down


def solution(mesh):
    return jax.shard_map(
        per_device,
        mesh=mesh,
        in_specs=(
            P("expert", "tensor"),
            P("expert", "tensor"),
            P("expert", None),
            P("expert", None),
            P("expert", "tensor", None),
            P("expert", "tensor", None),
            P("expert", "tensor", None),
        ),
        out_specs=(P("expert", "tensor"), P("expert", None), P("expert", "tensor", None)),
        check_vma=False,
    )
```

```python
import jax
import jax.numpy as jnp
from jax import lax
from jax.experimental import pallas as pl
from jax.experimental.pallas import tpu as pltpu
from jax.sharding import PartitionSpec as P

F32 = jnp.float32
BF16 = jnp.bfloat16
I32 = jnp.int32

EXPERTS = 16
CHIPS = 16
SIDE = 4
CAP = 20
SLOTS = EXPERTS * CAP
WIDE = 384
TOK = 64
TOP = 4
FEAT = 96
HID = 168
D = 3072
BLOCK = 32


def iota(shape, dim):
    return lax.broadcasted_iota(I32, shape, dim)


def flag(condition):
    return jnp.where(condition, 1.0, 0.0).astype(F32)


def hot(condition):
    return flag(condition).astype(BF16)


def dot(a, b):
    return jnp.dot(a, b, preferred_element_type=F32)


def dot_first(a, b):
    return lax.dot_general(a, b, (((0,), (0,)), ((), ())), preferred_element_type=F32)


def dot_last(a, b):
    return lax.dot_general(a, b, (((1,), (1,)), ((), ())), preferred_element_type=F32)


def expert_of(slot):
    return lax.shift_right_logical(slot * 3277, 16)


def params(mib, **kw):
    return pltpu.CompilerParams(vmem_limit_bytes=mib * 1024 * 1024, **kw)


def cost(flops):
    return pl.CostEstimate(flops=int(flops), bytes_accessed=4 << 20, transcendentals=0)


def pack_kernel(routes_hbm, probs_hbm, x_hbm, dy_hbm, out_ref, row_ref, routes_ref, probs_ref, x_ref, dy_ref, sems):
    pairs = ((routes_hbm, routes_ref), (probs_hbm, probs_ref), (x_hbm, x_ref), (dy_hbm, dy_ref))
    loads = [pltpu.make_async_copy(src, dst, sems.at[i]) for i, (src, dst) in enumerate(pairs)]
    for load in loads:
        load.start()
    for load in loads:
        load.wait()
    routes = routes_ref[...]
    probs = probs_ref[...].astype(F32)
    experts = iota((EXPERTS, TOK), 0)
    hits = [routes[k : k + 1, :] == experts for k in range(TOP)]
    member = sum(flag(h) for h in hits)
    weight = sum(jnp.where(hits[k], probs[k : k + 1, :], 0.0) for k in range(TOP))
    upper = hot(iota((TOK, TOK), 0) < iota((TOK, TOK), 1))
    count = dot(member.astype(BF16), upper)
    place = jnp.where(member > 0.5, count, -1.0)
    target = count + (experts * BLOCK).astype(F32)
    rows_of = [jnp.sum(jnp.where(hits[k], target, 0.0), axis=0, keepdims=True) for k in range(TOP)]
    kth = iota((8, TOK), 0)
    row_ref[...] = sum(jnp.where(kth == k, rows_of[k], 0.0) for k in range(TOP)).astype(I32)

    rows = EXPERTS * BLOCK
    expand = hot(lax.shift_right_logical(iota((rows, EXPERTS), 0), 5) == iota((rows, EXPERTS), 1))
    place_rows = dot(expand, place.astype(BF16))
    weight_rows = dot(expand, weight.astype(BF16))
    s_int = iota((rows, TOK), 0) & (BLOCK - 1)
    s = s_int.astype(F32)
    tail = (s_int >= CAP) & (s_int < 30)
    main = flag((place_rows == s) & (s_int < CAP))
    left = hot((place_rows == s - 20.0) & tail)
    right = hot((place_rows == s - 10.0) & tail)

    x = x_ref[...]
    dy = dy_ref[...]
    f = iota((FEAT, 128), 0)
    lane = iota((FEAT, 128), 1)
    b_main = dot(x, hot(lane == f)) + dot(dy, hot((lane == f + 96) & (f < 32)))
    b_left = dot(dy, hot((lane == f - 32) & (f >= 32)))
    b_right = dot(dy, hot((lane == f + 32) & (f >= 32)))

    prob_col = jnp.sum(main * weight_rows, axis=1, keepdims=True)
    s_lane = iota((rows, 128), 0) & (BLOCK - 1)
    prob_wide = jnp.where(s_lane == iota((rows, 128), 1), prob_col, 0.0).astype(BF16)
    gather = hot(lax.shift_right_logical(iota((EXPERTS, rows), 1), 5) == iota((EXPERTS, rows), 0))
    prob_block = dot(gather, prob_wide).astype(BF16)
    at_30 = hot(iota((rows, EXPERTS), 0) == iota((rows, EXPERTS), 1) * BLOCK + 30)

    out = (
        dot(main.astype(BF16), b_main.astype(BF16))
        + dot(left, b_left.astype(BF16))
        + dot(right, b_right.astype(BF16))
        + dot(at_30, prob_block)
    )
    out_ref[...] = out.astype(BF16).reshape(EXPERTS, BLOCK, 128)


def spread_kernel(got_ref, out_ref, prob_ref):
    rows = EXPERTS * BLOCK
    got = got_ref[...].reshape(rows, 128)
    n = iota((1, WIDE), 1)
    e_x = expert_of(n)
    s_x = n - e_x * CAP
    to_x = jnp.where(n < SLOTS, e_x * BLOCK + s_x, -1)
    slot = jnp.where(n < 128, n + 192, n - 128)
    e_d = expert_of(slot)
    s_d = slot - e_d * CAP
    live = n >= 64
    to_d = jnp.where(live, e_d * BLOCK + s_d, -1)
    to_left = jnp.where(live & (s_d < 10), e_d * BLOCK + 20 + s_d, -1)
    to_right = jnp.where(live & (s_d >= 10), e_d * BLOCK + 10 + s_d, -1)
    r = iota((rows, WIDE), 0)
    part_x = dot_first(got, hot(r == to_x))
    part_d = dot_first(got, hot(r == to_d))
    part_l = dot_first(got, hot(r == to_left))
    part_r = dot_first(got, hot(r == to_right))
    x_t = part_x[0:FEAT]
    d_t = jnp.concatenate([part_d[96:128], part_l[0:64] + part_r[64:128]], axis=0)
    first = x_t[:, 0:256].astype(BF16)
    middle = (x_t[:, 256:384] + d_t[:, 0:128]).astype(BF16)
    last = d_t[:, 128:384].astype(BF16)
    for j in range(SIDE):
        out_ref[j, :, 0:256] = first
        out_ref[j, :, 256:384] = middle
        out_ref[j, :, 384:640] = last

    pick = hot(iota((EXPERTS, rows), 1) == iota((EXPERTS, rows), 0) * BLOCK + 30)
    per_expert = dot(pick, got).astype(BF16)
    wide = dot(per_expert, hot(iota((128, WIDE), 0) == s_x))
    probs = jnp.sum(jnp.where(iota((EXPERTS, WIDE), 0) == e_x, wide, 0.0), axis=0, keepdims=True)
    prob_ref[...] = jnp.broadcast_to(probs, (8, WIDE))


def score_rows(scores):
    row = iota((16, 128), 0)
    return (
        jnp.where(row == 0, scores[:, 0:128], 0.0)
        + jnp.where(row == 1, scores[:, 128:256], 0.0)
        + jnp.where(row == 2, scores[:, 256:384], 0.0)
    )


def split_rows(scores):
    high = scores.astype(BF16).astype(F32)
    low = (scores - high).astype(BF16).astype(F32)
    return (high + pltpu.roll(low, 3, 0)).astype(BF16)


def squeeze(piece):
    last = piece[:, 256:384]
    lane = iota((48, 128), 1)
    both = jnp.where(lane < 64, last[0:48], pltpu.roll(last[48:96], 64, 1))
    return piece[:, 0:128], piece[:, 128:256], both


def this_core():
    return lax.rem(lax.axis_index("tensor"), 2)


def relay_kernel(got_ref, out_ref):
    for j in range(SIDE):
        out_ref[j] = got_ref[...]


def chip_of(i, core):
    return jnp.where(core == 0, i, (i % SIDE) * SIDE + i // SIDE)


def turn_kernel(
    own_ref, gate_ref, up_ref, down_ref, rows_ref, gate_t_ref, up_t_ref, far_ref, near_pre_ref, near_ref
):
    core = this_core()
    first = core == 0
    for i in range(CHIPS):
        rows_ref[chip_of(i, core), core] = own_ref[i // SIDE, i % SIDE]
    for w, weight_ref in enumerate((gate_ref, up_ref, down_ref)):
        for q in range(4):
            wide = weight_ref[0, :, pl.ds(q * 768, 768)]
            cut = [wide[:, 96 * p : 96 * p + 96] for p in range(8)]
            even = jnp.concatenate(cut[0::2], axis=1)
            odd = jnp.concatenate(cut[1::2], axis=1)
            near = jnp.where(first, even, odd)
            far = jnp.where(first, odd, even)
            at = pl.ds(q * 384, 384)
            near_ref[w, :, at] = near
            far_ref[w, :, at] = far
            if w < 2:
                turned_ref = (gate_t_ref, up_t_ref)[w]
                turned_ref[0, pl.ds(q * 4, 4)] = far.T.reshape(4, FEAT, HID)
                turned_ref[1, pl.ds(q * 4, 4)] = near.T.reshape(4, FEAT, HID)
    rows = rows_ref[:, core].reshape(D // 2, 640)
    near_pre_ref[0] = dot(near_ref[0], rows[:, 0:384])
    near_pre_ref[1] = dot(near_ref[1], rows[:, 0:384])
    near_pre_ref[2] = dot(near_ref[2], rows[:, 256:640])


def input_grads(turned, gate_t_ref, up_t_ref, grad_gate, grad_up, out_ref):
    for i in range(0, CHIPS, 4):
        part = pl.ds(i, 4)
        sums = dot(gate_t_ref[turned, part].reshape(384, HID), grad_gate)
        sums = sums + dot(up_t_ref[turned, part].reshape(384, HID), grad_up)
        for j in range(4):
            a, b, c = squeeze(sums[96 * j : 96 * j + 96])
            out_ref[i + j, 0:96] = a.astype(out_ref.dtype)
            out_ref[i + j, 96:192] = b.astype(out_ref.dtype)
            out_ref[i + j, 192:240] = c.astype(out_ref.dtype)


def middle_kernel(
    rows_in_ref, other_ref, far_ref, near_pre_ref, prob_ref, gate_t_ref, up_t_ref, rows_ref, send_ref, score_ref, hid_ref
):
    del rows_in_ref
    core = this_core()
    for i in range(CHIPS):
        rows_ref[chip_of(i, 1 - core), 1 - core] = other_ref[i // SIDE, i % SIDE]
    rows = rows_ref[:, 1 - core].reshape(D // 2, 640)
    x_t = rows[:, 0:384]
    dy_t = rows[:, 256:640]
    pre_gate = near_pre_ref[0] + dot(far_ref[0], x_t)
    pre_up = near_pre_ref[1] + dot(far_ref[1], x_t)
    raw = near_pre_ref[2] + dot(far_ref[2], dy_t)
    back = jnp.concatenate([raw[:, 128:384], pltpu.roll(raw[:, 0:128], 64, 1)], axis=1)
    live = iota((1, WIDE), 1) < SLOTS
    back = jnp.where(live, back, 0.0)
    probs = prob_ref[0:1, :]
    sig = jax.nn.sigmoid(pre_gate)
    silu = pre_gate * sig
    hidden = (silu * pre_up).astype(BF16).astype(F32)
    scores = score_rows(jnp.sum(hidden * back, axis=0, keepdims=True))
    scaled = jnp.where(live, probs * hidden, 0.0)
    back_p = probs * back
    grad_gate = jnp.where(live, back_p * pre_up * sig * (1.0 + pre_gate * (1.0 - sig)), 0.0).astype(BF16)
    grad_up = (back_p * silu).astype(BF16)
    input_grads(0, gate_t_ref, up_t_ref, grad_gate, grad_up, send_ref)
    parts = split_rows(scores)
    for j in range(CHIPS):
        send_ref[j, 240:256] = parts
    score_ref[...] = scores
    scaled = jnp.concatenate([pltpu.roll(scaled[:, 256:384], 64, 1), scaled[:, 0:256]], axis=1)
    hid_ref[0] = scaled.astype(BF16)
    hid_ref[1] = grad_gate
    hid_ref[2] = grad_up


def rest_kernel(rows_ref, hid_ref, gate_t_ref, up_t_ref, keep_ref, d_down_ref):
    d_down_ref[0] = dot_last(hid_ref[0], rows_ref[...].reshape(D, 640)[:, 256:640]).astype(BF16)
    input_grads(1, gate_t_ref, up_t_ref, hid_ref[1], hid_ref[2], keep_ref)


def join_kernel(keep_ref, score_ref, got_ref, out_ref):
    got = got_ref[0, 240:256].astype(F32)
    row = iota((16, 128), 0)
    total = score_ref[...] + got + pltpu.roll(got, 13, 0)
    parts = split_rows(jnp.where(row < 3, total, 0.0))
    for j in range(CHIPS):
        out_ref[j, 0:240] = (keep_ref[j, 0:240] + got_ref[j, 0:240].astype(F32)).astype(BF16)
        out_ref[j, 240:256] = parts


def fold_kernel(got_ref, out_ref):
    total = got_ref[0].astype(F32)
    for j in range(1, CHIPS):
        total = total + got_ref[j].astype(F32)
    both = total[192:240]
    lane = iota((48, 128), 1)
    last = jnp.concatenate(
        [jnp.where(lane < 64, both, 0.0), jnp.where(lane < 64, pltpu.roll(both, 64, 1), 0.0)], axis=0
    )
    grads = jnp.concatenate([total[0:96], total[96:192], last], axis=1)
    tail = total[240:256]
    score = tail + pltpu.roll(tail, 13, 0)
    wide = jnp.concatenate([score[0:1], score[1:2], score[2:3]], axis=1)
    high = wide.astype(BF16).astype(F32)
    low = wide - high
    row = iota((32, WIDE), 0)
    extra = jnp.where(row == 0, high, 0.0) + jnp.where(row == 1, low, 0.0)
    table = jnp.concatenate([grads, extra], axis=0).astype(BF16)
    n = iota((1, WIDE), 1)
    e = expert_of(n)
    to = jnp.where(n < SLOTS, e * BLOCK + (n - e * CAP), -1)
    pick = hot(iota((EXPERTS * BLOCK, WIDE), 0) == to)
    out_ref[...] = dot_last(pick, table).astype(BF16).reshape(EXPERTS, BLOCK, 128)


def combine_kernel(got_ref, row_ref, d_tokens_ref, d_probs_ref):
    rows = EXPERTS * BLOCK
    got = got_ref[...].reshape(rows, 128)
    r = iota((rows, TOK), 0)
    picks = [flag(r == row_ref[k : k + 1, :]) for k in range(TOP)]
    d_tokens_ref[...] = dot_first(sum(picks).astype(BF16), got)[:, 0:FEAT].astype(BF16)
    lane = iota((rows, 128), 1)
    score = jnp.where((lane == 96) | (lane == 97), got.astype(F32), 0.0)
    score = jnp.sum(score, axis=1, keepdims=True)
    for k in range(TOP):
        d_probs_ref[k : k + 1, :] = jnp.sum(picks[k] * score, axis=0, keepdims=True)


def struct(*shape, dtype):
    return jax.ShapeDtypeStruct(shape, dtype)


SAME_CORE = [[2 * j + core for j in range(CHIPS)] for core in range(2)]

LINES = [
    [[2 * (SIDE * y + x) for x in range(SIDE)] for y in range(SIDE)],
    [[2 * (SIDE * y + x) + 1 for y in range(SIDE)] for x in range(SIDE)],
    [[2 * (SIDE * y + x) for y in range(SIDE)] for x in range(SIDE)],
    [[2 * (SIDE * y + x) + 1 for x in range(SIDE)] for y in range(SIDE)],
]
OTHER_CORE = [(i, i ^ 1) for i in range(2 * CHIPS)]


def per_device(tokens, grad_out, probs, routes, gate_weight, up_weight, down_weight):
    packed, row_of = pl.pallas_call(
        pack_kernel,
        out_shape=(pltpu.VMEM((EXPERTS, BLOCK, 128), BF16), pltpu.VMEM((8, TOK), I32)),
        in_specs=[pl.BlockSpec(memory_space=pltpu.HBM)] * 4,
        scratch_shapes=[
            pltpu.VMEM((TOP, TOK), I32),
            pltpu.VMEM((TOP, TOK), BF16),
            pltpu.VMEM((TOK, FEAT), BF16),
            pltpu.VMEM((TOK, FEAT), BF16),
            pltpu.SemaphoreType.DMA((4,)),
        ],
        compiler_params=params(60),
        name="pack",
    )(routes.T, probs.T, tokens, grad_out)
    got = lax.all_to_all(packed, "expert", 0, 0, tiled=True)
    copies, prob_rows = pl.pallas_call(
        spread_kernel,
        out_shape=(struct(SIDE, FEAT, 640, dtype=BF16), struct(8, WIDE, dtype=F32)),
        compiler_params=params(16),
        name="spread",
    )(got)
    line = lax.all_to_all(copies, "tensor", 0, 0, tiled=True, axis_index_groups=LINES[0] + LINES[1])
    lines = pl.pallas_call(
        relay_kernel,
        out_shape=struct(SIDE, SIDE, FEAT, 640, dtype=BF16),
        compiler_params=params(16),
        name="relay",
    )(line)
    own = lax.all_to_all(lines, "tensor", 0, 0, tiled=True, axis_index_groups=LINES[2] + LINES[3])
    other = lax.ppermute(own, "tensor", OTHER_CORE)
    rows, gate_t, up_t, far, near_pre = pl.pallas_call(
        turn_kernel,
        out_shape=(
            struct(CHIPS, 2, FEAT, 640, dtype=BF16),
            struct(2, CHIPS, FEAT, HID, dtype=BF16),
            struct(2, CHIPS, FEAT, HID, dtype=BF16),
            struct(3, HID, D // 2, dtype=BF16),
            struct(3, HID, WIDE, dtype=F32),
        ),
        scratch_shapes=[pltpu.VMEM((3, HID, D // 2), BF16)],
        compiler_params=params(24),
        cost_estimate=cost(8e9),
        name="turn",
    )(own, gate_weight, up_weight, down_weight)
    rows, send, score, hid = pl.pallas_call(
        middle_kernel,
        out_shape=(
            struct(CHIPS, 2, FEAT, 640, dtype=BF16),
            struct(CHIPS, 256, 128, dtype=BF16),
            struct(16, 128, dtype=F32),
            struct(3, HID, WIDE, dtype=BF16),
        ),
        input_output_aliases={0: 0},
        compiler_params=params(24),
        cost_estimate=cost(4e9),
        name="middle",
    )(rows, other, far, near_pre, prob_rows, gate_t, up_t)
    partner = lax.ppermute(send, "tensor", OTHER_CORE)
    keep, d_down = pl.pallas_call(
        rest_kernel,
        out_shape=(struct(CHIPS, 240, 128, dtype=F32), struct(1, HID, D, dtype=BF16)),
        compiler_params=params(20),
        cost_estimate=cost(4e9),
        name="rest",
    )(rows, hid, gate_t, up_t)
    joined = pl.pallas_call(
        join_kernel,
        out_shape=struct(CHIPS, 256, 128, dtype=BF16),
        compiler_params=params(16),
        name="join",
    )(keep, score, partner)
    shares = lax.all_to_all(joined, "tensor", 0, 0, tiled=True, axis_index_groups=SAME_CORE)
    folded = pl.pallas_call(
        fold_kernel,
        out_shape=struct(EXPERTS, BLOCK, 128, dtype=BF16),
        compiler_params=params(16),
        name="fold",
    )(shares)
    back = lax.all_to_all(folded, "expert", 0, 0, tiled=True)
    d_tokens, d_probs = pl.pallas_call(
        combine_kernel,
        out_shape=(struct(TOK, FEAT, dtype=BF16), struct(TOP, TOK, dtype=F32)),
        compiler_params=params(16),
        name="combine",
    )(back, row_of)
    return d_tokens, d_probs.T, d_down


def solution(mesh):
    return jax.shard_map(
        per_device,
        mesh=mesh,
        in_specs=(
            P("expert", "tensor"),
            P("expert", "tensor"),
            P("expert", None),
            P("expert", None),
            P("expert", "tensor", None),
            P("expert", "tensor", None),
            P("expert", "tensor", None),
        ),
        out_specs=(P("expert", "tensor"), P("expert", None), P("expert", "tensor", None)),
        check_vma=False,
    )
```

```python
import jax
import jax.numpy as jnp
from jax import lax
from jax.experimental import pallas as pl
from jax.experimental.pallas import tpu as pltpu
from jax.sharding import PartitionSpec as P

F32 = jnp.float32
BF16 = jnp.bfloat16
I32 = jnp.int32

EXPERTS = 16
CHIPS = 16
SIDE = 4
CAP = 20
SLOTS = EXPERTS * CAP
WIDE = 384
TOK = 64
TOP = 4
FEAT = 96
HID = 168
D = 3072
BLOCK = 32
BACK = 16


def iota(shape, dim):
    return lax.broadcasted_iota(I32, shape, dim)


def flag(condition):
    return jnp.where(condition, 1.0, 0.0).astype(F32)


def hot(condition):
    return flag(condition).astype(BF16)


def dot(a, b):
    return jnp.dot(a, b, preferred_element_type=F32)


def dot_first(a, b):
    return lax.dot_general(a, b, (((0,), (0,)), ((), ())), preferred_element_type=F32)


def dot_last(a, b):
    return lax.dot_general(a, b, (((1,), (1,)), ((), ())), preferred_element_type=F32)


def expert_of(slot):
    return lax.shift_right_logical(slot * 3277, 16)


def params(mib, **kw):
    return pltpu.CompilerParams(vmem_limit_bytes=mib * 1024 * 1024, **kw)


def cost(flops):
    return pl.CostEstimate(flops=int(flops), bytes_accessed=4 << 20, transcendentals=0)


def pack_kernel(routes_hbm, probs_hbm, x_hbm, dy_hbm, out_ref, row_ref, routes_ref, probs_ref, x_ref, dy_ref, sems):
    pairs = ((routes_hbm, routes_ref), (probs_hbm, probs_ref), (x_hbm, x_ref), (dy_hbm, dy_ref))
    loads = [pltpu.make_async_copy(src, dst, sems.at[i]) for i, (src, dst) in enumerate(pairs)]
    for load in loads:
        load.start()
    for load in loads:
        load.wait()
    routes = routes_ref[...]
    probs = probs_ref[...].astype(F32)
    experts = iota((EXPERTS, TOK), 0)
    hits = [routes[k : k + 1, :] == experts for k in range(TOP)]
    member = sum(flag(h) for h in hits)
    weight = sum(jnp.where(hits[k], probs[k : k + 1, :], 0.0) for k in range(TOP))
    upper = hot(iota((TOK, TOK), 0) < iota((TOK, TOK), 1))
    count = dot(member.astype(BF16), upper)
    place = jnp.where(member > 0.5, count, -1.0)
    target = count + (experts * BLOCK).astype(F32)
    rows_of = [jnp.sum(jnp.where(hits[k], target, 0.0), axis=0, keepdims=True) for k in range(TOP)]
    kth = iota((8, TOK), 0)
    row_ref[...] = sum(jnp.where(kth == k, rows_of[k], 0.0) for k in range(TOP)).astype(I32)

    rows = EXPERTS * BLOCK
    expand = hot(lax.shift_right_logical(iota((rows, EXPERTS), 0), 5) == iota((rows, EXPERTS), 1))
    place_rows = dot(expand, place.astype(BF16))
    s_int = iota((rows, TOK), 0) & (BLOCK - 1)
    s = s_int.astype(F32)
    tail = (s_int >= CAP) & (s_int < 30)
    main = hot((place_rows == s) & (s_int < CAP))
    left = hot((place_rows == s - 20.0) & tail)
    right = hot((place_rows == s - 10.0) & tail)

    x = x_ref[...]
    dy = dy_ref[...]
    f = iota((FEAT, 128), 0)
    lane = iota((FEAT, 128), 1)
    b_main = dot(x, hot(lane == f)) + dot(dy, hot((lane == f + 96) & (f < 32)))
    b_left = dot(dy, hot((lane == f - 32) & (f >= 32)))
    b_right = dot(dy, hot((lane == f + 32) & (f >= 32)))

    lane_e = iota((EXPERTS, 128), 1)
    prob_block = jnp.zeros((EXPERTS, 128), F32)
    for j in range(CAP):
        column = jnp.sum(jnp.where(place == float(j), weight, 0.0), axis=1, keepdims=True)
        prob_block = jnp.where(lane_e == j, column, prob_block)
    prob_block = prob_block.astype(BF16)
    at_30 = hot(iota((rows, EXPERTS), 0) == iota((rows, EXPERTS), 1) * BLOCK + 30)

    out = (
        dot(main, b_main.astype(BF16))
        + dot(left, b_left.astype(BF16))
        + dot(right, b_right.astype(BF16))
        + dot(at_30, prob_block)
    )
    out_ref[...] = out.astype(BF16).reshape(EXPERTS, BLOCK, 128)


def spread_kernel(got_ref, out_ref, prob_ref):
    rows = EXPERTS * BLOCK
    got = got_ref[...].reshape(rows, 128)
    n = iota((1, WIDE), 1)
    e_x = expert_of(n)
    s_x = n - e_x * CAP
    to_x = jnp.where(n < SLOTS, e_x * BLOCK + s_x, -1)
    slot = jnp.where(n < 128, n + 192, n - 128)
    e_d = expert_of(slot)
    s_d = slot - e_d * CAP
    live = n >= 64
    to_d = jnp.where(live, e_d * BLOCK + s_d, -1)
    to_left = jnp.where(live & (s_d < 10), e_d * BLOCK + 20 + s_d, -1)
    to_right = jnp.where(live & (s_d >= 10), e_d * BLOCK + 10 + s_d, -1)
    r = iota((rows, WIDE), 0)
    part_x = dot_first(got, hot(r == to_x))
    part_d = dot_first(got, hot(r == to_d))
    part_l = dot_first(got, hot(r == to_left))
    part_r = dot_first(got, hot(r == to_right))
    x_t = part_x[0:FEAT]
    d_t = jnp.concatenate([part_d[96:128], part_l[0:64] + part_r[64:128]], axis=0)
    first = x_t[:, 0:256].astype(BF16)
    middle = (x_t[:, 256:384] + d_t[:, 0:128]).astype(BF16)
    last = d_t[:, 128:384].astype(BF16)
    for j in range(SIDE):
        out_ref[j, :, 0:256] = first
        out_ref[j, :, 256:384] = middle
        out_ref[j, :, 384:640] = last

    pick = hot(iota((EXPERTS, rows), 1) == iota((EXPERTS, rows), 0) * BLOCK + 30)
    per_expert = dot(pick, got).astype(BF16)
    wide = dot(per_expert, hot(iota((128, WIDE), 0) == s_x))
    probs = jnp.sum(jnp.where(iota((EXPERTS, WIDE), 0) == e_x, wide, 0.0), axis=0, keepdims=True)
    prob_ref[...] = jnp.broadcast_to(probs, (8, WIDE))


def score_rows(scores):
    row = iota((16, 128), 0)
    return (
        jnp.where(row == 0, scores[:, 0:128], 0.0)
        + jnp.where(row == 1, scores[:, 128:256], 0.0)
        + jnp.where(row == 2, scores[:, 256:384], 0.0)
    )


def split_rows(scores):
    high = scores.astype(BF16).astype(F32)
    low = (scores - high).astype(BF16).astype(F32)
    return (high + pltpu.roll(low, 3, 0)).astype(BF16)


def squeeze(piece):
    last = piece[:, 256:384]
    lane = iota((48, 128), 1)
    both = jnp.where(lane < 64, last[0:48], pltpu.roll(last[48:96], 64, 1))
    return piece[:, 0:128], piece[:, 128:256], both


def this_core():
    return lax.rem(lax.axis_index("tensor"), 2)


def relay_kernel(got_ref, out_ref):
    for j in range(SIDE):
        out_ref[j] = got_ref[...]


def chip_of(i, core):
    return jnp.where(core == 0, i, (i % SIDE) * SIDE + i // SIDE)


def turn_kernel(
    own_ref, gate_ref, up_ref, down_ref, rows_ref, gate_t_ref, up_t_ref, far_ref, near_pre_ref, near_ref
):
    core = this_core()
    first = core == 0
    for i in range(CHIPS):
        rows_ref[chip_of(i, core), core] = own_ref[i // SIDE, i % SIDE]
    for w, weight_ref in enumerate((gate_ref, up_ref, down_ref)):
        for q in range(4):
            wide = weight_ref[0, :, pl.ds(q * 768, 768)]
            cut = [wide[:, 96 * p : 96 * p + 96] for p in range(8)]
            even = jnp.concatenate(cut[0::2], axis=1)
            odd = jnp.concatenate(cut[1::2], axis=1)
            near = jnp.where(first, even, odd)
            far = jnp.where(first, odd, even)
            at = pl.ds(q * 384, 384)
            near_ref[w, :, at] = near
            far_ref[w, :, at] = far
            if w < 2:
                turned_ref = (gate_t_ref, up_t_ref)[w]
                turned_ref[0, pl.ds(q * 4, 4)] = far.T.reshape(4, FEAT, HID)
                turned_ref[1, pl.ds(q * 4, 4)] = near.T.reshape(4, FEAT, HID)
    rows = rows_ref[:, core].reshape(D // 2, 640)
    near_pre_ref[0] = dot(near_ref[0], rows[:, 0:384])
    near_pre_ref[1] = dot(near_ref[1], rows[:, 0:384])
    near_pre_ref[2] = dot(near_ref[2], rows[:, 256:640])


def input_grads(turned, gate_t_ref, up_t_ref, grad_gate, grad_up, out_ref):
    for i in range(0, CHIPS, 4):
        part = pl.ds(i, 4)
        sums = dot(gate_t_ref[turned, part].reshape(384, HID), grad_gate)
        sums = sums + dot(up_t_ref[turned, part].reshape(384, HID), grad_up)
        for j in range(4):
            a, b, c = squeeze(sums[96 * j : 96 * j + 96])
            out_ref[i + j, 0:96] = a.astype(out_ref.dtype)
            out_ref[i + j, 96:192] = b.astype(out_ref.dtype)
            out_ref[i + j, 192:240] = c.astype(out_ref.dtype)


def middle_kernel(
    rows_in_ref, other_ref, far_ref, near_pre_ref, prob_ref, gate_t_ref, up_t_ref, rows_ref, send_ref, score_ref, hid_ref
):
    del rows_in_ref
    core = this_core()
    for i in range(CHIPS):
        rows_ref[chip_of(i, 1 - core), 1 - core] = other_ref[i // SIDE, i % SIDE]
    rows = rows_ref[:, 1 - core].reshape(D // 2, 640)
    x_t = rows[:, 0:384]
    dy_t = rows[:, 256:640]
    pre_gate = near_pre_ref[0] + dot(far_ref[0], x_t)
    pre_up = near_pre_ref[1] + dot(far_ref[1], x_t)
    raw = near_pre_ref[2] + dot(far_ref[2], dy_t)
    back = jnp.concatenate([raw[:, 128:384], pltpu.roll(raw[:, 0:128], 64, 1)], axis=1)
    live = iota((1, WIDE), 1) < SLOTS
    back = jnp.where(live, back, 0.0)
    probs = prob_ref[0:1, :]
    sig = jax.nn.sigmoid(pre_gate)
    silu = pre_gate * sig
    hidden = (silu * pre_up).astype(BF16).astype(F32)
    scores = score_rows(jnp.sum(hidden * back, axis=0, keepdims=True))
    scaled = jnp.where(live, probs * hidden, 0.0)
    back_p = probs * back
    grad_gate = jnp.where(live, back_p * pre_up * sig * (1.0 + pre_gate * (1.0 - sig)), 0.0).astype(BF16)
    grad_up = (back_p * silu).astype(BF16)
    input_grads(0, gate_t_ref, up_t_ref, grad_gate, grad_up, send_ref)
    parts = split_rows(scores)
    for j in range(CHIPS):
        send_ref[j, 240:256] = parts
    score_ref[...] = scores
    scaled = jnp.concatenate([pltpu.roll(scaled[:, 256:384], 64, 1), scaled[:, 0:256]], axis=1)
    hid_ref[0] = scaled.astype(BF16)
    hid_ref[1] = grad_gate
    hid_ref[2] = grad_up


def rest_kernel(rows_ref, hid_ref, gate_t_ref, up_t_ref, keep_ref, d_down_ref):
    d_down_ref[0] = dot_last(hid_ref[0], rows_ref[...].reshape(D, 640)[:, 256:640]).astype(BF16)
    input_grads(1, gate_t_ref, up_t_ref, hid_ref[1], hid_ref[2], keep_ref)


def join_kernel(keep_ref, score_ref, got_ref, out_ref):
    got = got_ref[0, 240:256].astype(F32)
    row = iota((16, 128), 0)
    total = score_ref[...] + got + pltpu.roll(got, 13, 0)
    parts = split_rows(jnp.where(row < 3, total, 0.0))
    for j in range(CHIPS):
        out_ref[j, 0:240] = (keep_ref[j, 0:240] + got_ref[j, 0:240].astype(F32)).astype(BF16)
        out_ref[j, 240:256] = parts


def fold_kernel(got_ref, out_ref):
    total = got_ref[0].astype(F32)
    for j in range(1, CHIPS):
        total = total + got_ref[j].astype(F32)
    both = total[192:240]
    lane = iota((48, 128), 1)
    last = jnp.concatenate(
        [jnp.where(lane < 64, both, 0.0), jnp.where(lane < 64, pltpu.roll(both, 64, 1), 0.0)], axis=0
    )
    grads = jnp.concatenate([total[0:96], total[96:192], last], axis=1)
    tail = total[240:256]
    score = tail + pltpu.roll(tail, 13, 0)
    wide = jnp.concatenate([score[0:1], score[1:2], score[2:3]], axis=1)
    high = wide.astype(BF16).astype(F32)
    low = wide - high
    n = iota((1, WIDE), 1)
    e = expert_of(n)
    slot = n - e * CAP
    base = jnp.where(n < SLOTS, e * BACK, -2 * BACK)
    r = iota((EXPERTS * BACK, WIDE), 0)
    upper = jnp.concatenate([grads, jnp.zeros((32, WIDE), F32)], axis=0).astype(BF16)
    out = dot_last(hot((r == base + slot) & (slot < BACK)), upper)
    for q in range(3):
        part = jnp.concatenate([jnp.zeros((FEAT, WIDE), F32), grads[32 * q : 32 * q + 32]], axis=0).astype(BF16)
        out = out + dot_last(hot((r == base + 3 * (slot - BACK) + q) & (slot >= BACK)), part)
    values = jnp.where(r == base + 12, high, 0.0) + jnp.where(r == base + 13, low, 0.0)
    out = out + dot_last(values.astype(BF16), hot(iota((128, WIDE), 0) == slot + FEAT))
    out_ref[...] = out.astype(BF16).reshape(EXPERTS, BACK, 128)


def combine_kernel(got_ref, row_ref, d_tokens_ref, d_probs_ref):
    rows = EXPERTS * BACK
    got = got_ref[...].reshape(rows, 128)
    r = iota((rows, TOK), 0)
    lane = iota((128, TOK), 0)
    pick = jnp.zeros((rows, TOK), F32)
    rest = [jnp.zeros((rows, TOK), F32) for _ in range(3)]
    own = iota((EXPERTS, rows), 1) - iota((EXPERTS, rows), 0) * BACK
    high = dot(hot(own == 12), got).astype(BF16)
    low = dot(hot(own == 13), got).astype(BF16)
    for k in range(TOP):
        at = row_ref[k : k + 1, :]
        e = lax.shift_right_logical(at, 5)
        slot = at & (BLOCK - 1)
        base = e * BACK
        pick = pick + flag((r == base + slot) & (slot < BACK))
        for q in range(3):
            rest[q] = rest[q] + flag((r == base + 3 * (slot - BACK) + q) & (slot >= BACK))
        mine = hot(iota((EXPERTS, TOK), 0) == e)
        score = dot_first(high, mine) + dot_first(low, mine)
        d_probs_ref[k : k + 1, :] = jnp.sum(jnp.where(lane == slot + FEAT, score, 0.0), axis=0, keepdims=True)
    total = dot_first(pick.astype(BF16), got)
    feature = iota((TOK, 128), 1)
    for q in range(3):
        part = pltpu.roll(dot_first(rest[q].astype(BF16), got), 32 + 32 * q, 1)
        total = total + jnp.where(lax.shift_right_logical(feature, 5) == q, part, 0.0)
    d_tokens_ref[...] = total[:, 0:FEAT].astype(BF16)


def struct(*shape, dtype):
    return jax.ShapeDtypeStruct(shape, dtype)


SAME_CORE = [[2 * j + core for j in range(CHIPS)] for core in range(2)]

LINES = [
    [[2 * (SIDE * y + x) for x in range(SIDE)] for y in range(SIDE)],
    [[2 * (SIDE * y + x) + 1 for y in range(SIDE)] for x in range(SIDE)],
    [[2 * (SIDE * y + x) for y in range(SIDE)] for x in range(SIDE)],
    [[2 * (SIDE * y + x) + 1 for x in range(SIDE)] for y in range(SIDE)],
]
OTHER_CORE = [(i, i ^ 1) for i in range(2 * CHIPS)]


def per_device(tokens, grad_out, probs, routes, gate_weight, up_weight, down_weight):
    packed, row_of = pl.pallas_call(
        pack_kernel,
        out_shape=(pltpu.VMEM((EXPERTS, BLOCK, 128), BF16), pltpu.VMEM((8, TOK), I32)),
        in_specs=[pl.BlockSpec(memory_space=pltpu.HBM)] * 4,
        scratch_shapes=[
            pltpu.VMEM((TOP, TOK), I32),
            pltpu.VMEM((TOP, TOK), BF16),
            pltpu.VMEM((TOK, FEAT), BF16),
            pltpu.VMEM((TOK, FEAT), BF16),
            pltpu.SemaphoreType.DMA((4,)),
        ],
        compiler_params=params(60),
        name="pack",
    )(routes.T, probs.T, tokens, grad_out)
    got = lax.all_to_all(packed, "expert", 0, 0, tiled=True)
    copies, prob_rows = pl.pallas_call(
        spread_kernel,
        out_shape=(struct(SIDE, FEAT, 640, dtype=BF16), struct(8, WIDE, dtype=F32)),
        compiler_params=params(16),
        name="spread",
    )(got)
    line = lax.all_to_all(copies, "tensor", 0, 0, tiled=True, axis_index_groups=LINES[0] + LINES[1])
    lines = pl.pallas_call(
        relay_kernel,
        out_shape=struct(SIDE, SIDE, FEAT, 640, dtype=BF16),
        compiler_params=params(16),
        name="relay",
    )(line)
    own = lax.all_to_all(lines, "tensor", 0, 0, tiled=True, axis_index_groups=LINES[2] + LINES[3])
    other = lax.ppermute(own, "tensor", OTHER_CORE)
    rows, gate_t, up_t, far, near_pre = pl.pallas_call(
        turn_kernel,
        out_shape=(
            struct(CHIPS, 2, FEAT, 640, dtype=BF16),
            struct(2, CHIPS, FEAT, HID, dtype=BF16),
            struct(2, CHIPS, FEAT, HID, dtype=BF16),
            struct(3, HID, D // 2, dtype=BF16),
            struct(3, HID, WIDE, dtype=F32),
        ),
        scratch_shapes=[pltpu.VMEM((3, HID, D // 2), BF16)],
        compiler_params=params(24),
        cost_estimate=cost(8e9),
        name="turn",
    )(own, gate_weight, up_weight, down_weight)
    rows, send, score, hid = pl.pallas_call(
        middle_kernel,
        out_shape=(
            struct(CHIPS, 2, FEAT, 640, dtype=BF16),
            struct(CHIPS, 256, 128, dtype=BF16),
            struct(16, 128, dtype=F32),
            struct(3, HID, WIDE, dtype=BF16),
        ),
        input_output_aliases={0: 0},
        compiler_params=params(24),
        cost_estimate=cost(4e9),
        name="middle",
    )(rows, other, far, near_pre, prob_rows, gate_t, up_t)
    partner = lax.ppermute(send, "tensor", OTHER_CORE)
    keep, d_down = pl.pallas_call(
        rest_kernel,
        out_shape=(struct(CHIPS, 240, 128, dtype=F32), struct(1, HID, D, dtype=BF16)),
        compiler_params=params(20),
        cost_estimate=cost(4e9),
        name="rest",
    )(rows, hid, gate_t, up_t)
    joined = pl.pallas_call(
        join_kernel,
        out_shape=struct(CHIPS, 256, 128, dtype=BF16),
        compiler_params=params(16),
        name="join",
    )(keep, score, partner)
    shares = lax.all_to_all(joined, "tensor", 0, 0, tiled=True, axis_index_groups=SAME_CORE)
    folded = pl.pallas_call(
        fold_kernel,
        out_shape=struct(EXPERTS, BACK, 128, dtype=BF16),
        compiler_params=params(16),
        name="fold",
    )(shares)
    back = lax.all_to_all(folded, "expert", 0, 0, tiled=True)
    d_tokens, d_probs = pl.pallas_call(
        combine_kernel,
        out_shape=(struct(TOK, FEAT, dtype=BF16), struct(TOP, TOK, dtype=F32)),
        compiler_params=params(16),
        name="combine",
    )(back, row_of)
    return d_tokens, d_probs.T, d_down


def solution(mesh):
    return jax.shard_map(
        per_device,
        mesh=mesh,
        in_specs=(
            P("expert", "tensor"),
            P("expert", "tensor"),
            P("expert", None),
            P("expert", None),
            P("expert", "tensor", None),
            P("expert", "tensor", None),
            P("expert", "tensor", None),
        ),
        out_specs=(P("expert", "tensor"), P("expert", None), P("expert", "tensor", None)),
        check_vma=False,
    )
```

```python
import jax
import jax.numpy as jnp
import ml_dtypes
import numpy as np
from jax import lax
from jax.experimental import pallas as pl
from jax.experimental.pallas import tpu as pltpu
from jax.sharding import PartitionSpec as P

F32 = jnp.float32
BF16 = jnp.bfloat16
I32 = jnp.int32

EXPERTS = 16
CHIPS = 16
SIDE = 4
CAP = 20
SLOTS = EXPERTS * CAP
WIDE = 384
TOK = 64
TOP = 4
FEAT = 96
HID = 168
D = 3072
BLOCK = 32
BACK = 16


def iota(shape, dim):
    return lax.broadcasted_iota(I32, shape, dim)


def flag(condition):
    return jnp.where(condition, 1.0, 0.0).astype(F32)


def hot(condition):
    return flag(condition).astype(BF16)


def dot(a, b):
    return jnp.dot(a, b, preferred_element_type=F32)


def dot_first(a, b):
    return lax.dot_general(a, b, (((0,), (0,)), ((), ())), preferred_element_type=F32)


def dot_last(a, b):
    return lax.dot_general(a, b, (((1,), (1,)), ((), ())), preferred_element_type=F32)


def expert_of(slot):
    return lax.shift_right_logical(slot * 3277, 16)


def params(mib, **kw):
    return pltpu.CompilerParams(vmem_limit_bytes=mib * 1024 * 1024, **kw)


def cost(flops):
    return pl.CostEstimate(flops=int(flops), bytes_accessed=4 << 20, transcendentals=0)


def pack_kernel(routes_hbm, probs_hbm, x_hbm, dy_hbm, out_ref, row_ref, routes_ref, probs_ref, x_ref, dy_ref, sems):
    pairs = ((routes_hbm, routes_ref), (probs_hbm, probs_ref), (x_hbm, x_ref), (dy_hbm, dy_ref))
    loads = [pltpu.make_async_copy(src, dst, sems.at[i]) for i, (src, dst) in enumerate(pairs)]
    for load in loads:
        load.start()
    for load in loads:
        load.wait()
    routes = routes_ref[...]
    probs = probs_ref[...].astype(F32)
    experts = iota((EXPERTS, TOK), 0)
    hits = [routes[k : k + 1, :] == experts for k in range(TOP)]
    member = sum(flag(h) for h in hits)
    weight = sum(jnp.where(hits[k], probs[k : k + 1, :], 0.0) for k in range(TOP))
    upper = hot(iota((TOK, TOK), 0) < iota((TOK, TOK), 1))
    count = dot(member.astype(BF16), upper)
    place = jnp.where(member > 0.5, count, -1.0)
    target = count + (experts * BLOCK).astype(F32)
    rows_of = [jnp.sum(jnp.where(hits[k], target, 0.0), axis=0, keepdims=True) for k in range(TOP)]
    kth = iota((8, TOK), 0)
    row_ref[...] = sum(jnp.where(kth == k, rows_of[k], 0.0) for k in range(TOP)).astype(I32)

    rows = EXPERTS * BLOCK
    expand = hot(lax.shift_right_logical(iota((rows, EXPERTS), 0), 5) == iota((rows, EXPERTS), 1))
    place_rows = dot(expand, place.astype(BF16))
    s_int = iota((rows, TOK), 0) & (BLOCK - 1)
    s = s_int.astype(F32)
    tail = (s_int >= CAP) & (s_int < 30)
    main = hot((place_rows == s) & (s_int < CAP))
    left = hot((place_rows == s - 20.0) & tail)
    right = hot((place_rows == s - 10.0) & tail)

    x = x_ref[...]
    dy = dy_ref[...]
    f = iota((FEAT, 128), 0)
    lane = iota((FEAT, 128), 1)
    b_main = dot(x, hot(lane == f)) + dot(dy, hot((lane == f + 96) & (f < 32)))
    b_left = dot(dy, hot((lane == f - 32) & (f >= 32)))
    b_right = dot(dy, hot((lane == f + 32) & (f >= 32)))

    lane_e = iota((EXPERTS, 128), 1)
    prob_block = jnp.zeros((EXPERTS, 128), F32)
    for j in range(CAP):
        column = jnp.sum(jnp.where(place == float(j), weight, 0.0), axis=1, keepdims=True)
        prob_block = jnp.where(lane_e == j, column, prob_block)
    prob_block = prob_block.astype(BF16)
    at_30 = hot(iota((rows, EXPERTS), 0) == iota((rows, EXPERTS), 1) * BLOCK + 30)

    out = (
        dot(main, b_main.astype(BF16))
        + dot(left, b_left.astype(BF16))
        + dot(right, b_right.astype(BF16))
        + dot(at_30, prob_block)
    )
    out_ref[...] = out.astype(BF16).reshape(EXPERTS, BLOCK, 128)


def fold_table():
    n = np.arange(WIDE)
    r = np.arange(EXPERTS * BACK)[:, None]
    e, s = n // CAP, n % CAP
    masks = [(r == e * BACK + s) & (s < BACK)]
    masks += [(r == e * BACK + 3 * (s - BACK) + q) & (s >= BACK) for q in range(3)]
    masks += [r == e * BACK + 12, r == e * BACK + 13]
    return (np.stack(masks) & (n < SLOTS)).astype(ml_dtypes.bfloat16)


def spread_kernel(got_ref, out_ref, prob_ref):
    rows = EXPERTS * BLOCK
    got = got_ref[...].reshape(rows, 128)
    n = iota((1, WIDE), 1)
    e_x = expert_of(n)
    s_x = n - e_x * CAP
    to_x = jnp.where(n < SLOTS, e_x * BLOCK + s_x, -1)
    slot = jnp.where(n < 128, n + 192, n - 128)
    e_d = expert_of(slot)
    s_d = slot - e_d * CAP
    live = n >= 64
    to_d = jnp.where(live, e_d * BLOCK + s_d, -1)
    to_left = jnp.where(live & (s_d < 10), e_d * BLOCK + 20 + s_d, -1)
    to_right = jnp.where(live & (s_d >= 10), e_d * BLOCK + 10 + s_d, -1)
    r = iota((rows, WIDE), 0)
    got_t = got.T
    part_x = dot(got_t, hot(r == to_x))
    part_d = dot(got_t, hot(r == to_d))
    both = hot(r == to_left + to_right + 1)
    mixed = dot(got_t, both)
    part_l = jnp.where(s_d < 10, mixed, 0.0)
    part_r = jnp.where(s_d < 10, 0.0, mixed)
    x_t = part_x[0:FEAT]
    d_t = jnp.concatenate([part_d[96:128], part_l[0:64] + part_r[64:128]], axis=0)
    first = x_t[:, 0:256].astype(BF16)
    middle = (x_t[:, 256:384] + d_t[:, 0:128]).astype(BF16)
    last = d_t[:, 128:384].astype(BF16)
    for j in range(SIDE):
        out_ref[j, :, 0:256] = first
        out_ref[j, :, 256:384] = middle
        out_ref[j, :, 384:640] = last

    pick = hot(iota((EXPERTS, rows), 1) == iota((EXPERTS, rows), 0) * BLOCK + 30)
    per_expert = dot(pick, got).astype(BF16)
    wide = dot(per_expert, hot(iota((128, WIDE), 0) == s_x))
    probs = jnp.sum(jnp.where(iota((EXPERTS, WIDE), 0) == e_x, wide, 0.0), axis=0, keepdims=True)
    prob_ref[...] = jnp.broadcast_to(probs, (8, WIDE))


def score_rows(scores):
    row = iota((16, 128), 0)
    return (
        jnp.where(row == 0, scores[:, 0:128], 0.0)
        + jnp.where(row == 1, scores[:, 128:256], 0.0)
        + jnp.where(row == 2, scores[:, 256:384], 0.0)
    )


def split_rows(scores):
    high = scores.astype(BF16).astype(F32)
    low = (scores - high).astype(BF16).astype(F32)
    return (high + pltpu.roll(low, 3, 0)).astype(BF16)


def squeeze(piece):
    last = piece[:, 256:384]
    lane = iota((48, 128), 1)
    both = jnp.where(lane < 64, last[0:48], pltpu.roll(last[48:96], 64, 1))
    return piece[:, 0:128], piece[:, 128:256], both


def this_core():
    return lax.rem(lax.axis_index("tensor"), 2)


def relay_kernel(got_ref, out_ref):
    for j in range(SIDE):
        out_ref[j] = got_ref[...]


def chip_of(i, core):
    return jnp.where(core == 0, i, (i % SIDE) * SIDE + i // SIDE)


def pick_routes(row_ref, pick_ref):
    places = row_ref[...].astype(F32).T.astype(I32)
    r = iota((TOK, EXPERTS * BACK), 1)
    picks = [jnp.zeros(r.shape, F32)] * 4
    for k in range(TOP):
        at = places[:, k : k + 1]
        slot = at & (BLOCK - 1)
        base = lax.shift_right_logical(at, 5) * BACK
        first = jnp.where(slot < BACK, base + slot, -1)
        later = jnp.where(slot < BACK, -3, base + 3 * (slot - BACK))
        picks[0] = picks[0] + flag(r == first)
        for q in range(3):
            picks[1 + q] = picks[1 + q] + flag(r == later + q)
    for q in range(4):
        pick_ref[q] = picks[q].astype(BF16)


def turn_kernel(
    own_ref,
    gate_ref,
    up_ref,
    down_ref,
    row_ref,
    rows_ref,
    gate_t_ref,
    up_t_ref,
    far_ref,
    near_pre_ref,
    pick_ref,
    near_ref,
):
    core = this_core()
    first = core == 0
    for i in range(CHIPS):
        rows_ref[chip_of(i, core), core] = own_ref[i // SIDE, i % SIDE]
    for w, weight_ref in enumerate((gate_ref, up_ref, down_ref)):
        for q in range(4):
            wide = weight_ref[0, :, pl.ds(q * 768, 768)]
            cut = [wide[:, 96 * p : 96 * p + 96] for p in range(8)]
            even = jnp.concatenate(cut[0::2], axis=1)
            odd = jnp.concatenate(cut[1::2], axis=1)
            near = jnp.where(first, even, odd)
            far = jnp.where(first, odd, even)
            at = pl.ds(q * 384, 384)
            near_ref[w, :, at] = near
            far_ref[w, :, at] = far
            if w < 2:
                turned_ref = (gate_t_ref, up_t_ref)[w]
                turned_ref[0, pl.ds(q * 4, 4)] = far.T.reshape(4, FEAT, HID)
                turned_ref[1, pl.ds(q * 4, 4)] = near.T.reshape(4, FEAT, HID)
    rows = rows_ref[:, core].reshape(D // 2, 640)
    near_pre_ref[0] = dot(near_ref[0], rows[:, 0:384])
    near_pre_ref[1] = dot(near_ref[1], rows[:, 0:384])
    near_pre_ref[2] = dot(near_ref[2], rows[:, 256:640])
    pick_routes(row_ref, pick_ref)


def input_grads(turned, gate_t_ref, up_t_ref, grad_gate, grad_up, out_ref):
    for i in range(0, CHIPS, 4):
        part = pl.ds(i, 4)
        sums = dot(gate_t_ref[turned, part].reshape(384, HID), grad_gate)
        sums = sums + dot(up_t_ref[turned, part].reshape(384, HID), grad_up)
        for j in range(4):
            a, b, c = squeeze(sums[96 * j : 96 * j + 96])
            out_ref[i + j, 0:96] = a.astype(out_ref.dtype)
            out_ref[i + j, 96:192] = b.astype(out_ref.dtype)
            out_ref[i + j, 192:240] = c.astype(out_ref.dtype)


def middle_kernel(
    rows_in_ref, other_ref, far_ref, near_pre_ref, prob_ref, gate_t_ref, up_t_ref, rows_ref, send_ref, score_ref, hid_ref
):
    del rows_in_ref
    core = this_core()
    for i in range(CHIPS):
        rows_ref[chip_of(i, 1 - core), 1 - core] = other_ref[i // SIDE, i % SIDE]
    rows = rows_ref[:, 1 - core].reshape(D // 2, 640)
    x_t = rows[:, 0:384]
    dy_t = rows[:, 256:640]
    pre_gate = near_pre_ref[0] + dot(far_ref[0], x_t)
    pre_up = near_pre_ref[1] + dot(far_ref[1], x_t)
    raw = near_pre_ref[2] + dot(far_ref[2], dy_t)
    back = jnp.concatenate([raw[:, 128:384], pltpu.roll(raw[:, 0:128], 64, 1)], axis=1)
    live = iota((1, WIDE), 1) < SLOTS
    back = jnp.where(live, back, 0.0)
    probs = prob_ref[0:1, :]
    sig = jax.nn.sigmoid(pre_gate)
    silu = pre_gate * sig
    hidden = (silu * pre_up).astype(BF16).astype(F32)
    scores = score_rows(jnp.sum(hidden * back, axis=0, keepdims=True))
    scaled = jnp.where(live, probs * hidden, 0.0)
    back_p = probs * back
    grad_gate = jnp.where(live, back_p * pre_up * sig * (1.0 + pre_gate * (1.0 - sig)), 0.0).astype(BF16)
    grad_up = (back_p * silu).astype(BF16)
    input_grads(0, gate_t_ref, up_t_ref, grad_gate, grad_up, send_ref)
    parts = split_rows(scores)
    for j in range(CHIPS):
        send_ref[j, 240:256] = parts
    score_ref[...] = scores
    scaled = jnp.concatenate([pltpu.roll(scaled[:, 256:384], 64, 1), scaled[:, 0:256]], axis=1)
    hid_ref[0] = scaled.astype(BF16)
    hid_ref[1] = grad_gate
    hid_ref[2] = grad_up


def rest_kernel(rows_ref, hid_ref, gate_t_ref, up_t_ref, keep_ref, d_down_ref):
    d_down_ref[0] = dot_last(hid_ref[0], rows_ref[...].reshape(D, 640)[:, 256:640]).astype(BF16)
    input_grads(1, gate_t_ref, up_t_ref, hid_ref[1], hid_ref[2], keep_ref)


def join_kernel(keep_ref, score_ref, got_ref, out_ref):
    got = got_ref[0, 240:256].astype(F32)
    row = iota((16, 128), 0)
    total = score_ref[...] + got + pltpu.roll(got, 13, 0)
    parts = split_rows(jnp.where(row < 3, total, 0.0))
    for j in range(CHIPS):
        out_ref[j, 0:240] = (keep_ref[j, 0:240] + got_ref[j, 0:240].astype(F32)).astype(BF16)
        out_ref[j, 240:256] = parts


def fold_kernel(got_ref, table_ref, out_ref):
    total = got_ref[0].astype(F32)
    for j in range(1, CHIPS):
        total = total + got_ref[j].astype(F32)
    both = total[192:240]
    lane = iota((48, 128), 1)
    last = jnp.concatenate(
        [jnp.where(lane < 64, both, 0.0), jnp.where(lane < 64, pltpu.roll(both, 64, 1), 0.0)], axis=0
    )
    grads = jnp.concatenate([total[0:96], total[96:192], last], axis=1)
    tail = total[240:256]
    score = tail + pltpu.roll(tail, 13, 0)
    wide = jnp.concatenate([score[0:1], score[1:2], score[2:3]], axis=1)
    high = wide.astype(BF16).astype(F32)
    low = wide - high
    n = iota((1, WIDE), 1)
    e = expert_of(n)
    slot = n - e * CAP
    upper = jnp.concatenate([grads, jnp.zeros((32, WIDE), F32)], axis=0).astype(BF16)
    out = dot_last(table_ref[0], upper)
    for q in range(3):
        part = jnp.concatenate([jnp.zeros((FEAT, WIDE), F32), grads[32 * q : 32 * q + 32]], axis=0).astype(BF16)
        out = out + dot_last(table_ref[1 + q], part)
    values = table_ref[4].astype(F32) * high + table_ref[5].astype(F32) * low
    out = out + dot_last(values.astype(BF16), hot(iota((128, WIDE), 0) == slot + FEAT))
    out_ref[...] = out.astype(BF16).reshape(EXPERTS, BACK, 128)


def combine_kernel(got_ref, row_ref, pick_ref, d_tokens_ref, d_probs_ref):
    rows = EXPERTS * BACK
    got = got_ref[...].reshape(rows, 128)
    total = dot(pick_ref[0], got)
    feature = iota((TOK, 128), 1)
    for q in range(3):
        part = pltpu.roll(dot(pick_ref[1 + q], got), 32 + 32 * q, 1)
        total = total + jnp.where(lax.shift_right_logical(feature, 5) == q, part, 0.0)
    d_tokens_ref[...] = total[:, 0:FEAT].astype(BF16)
    lane = iota((128, TOK), 0)
    own = iota((EXPERTS, rows), 1) - iota((EXPERTS, rows), 0) * BACK
    high = dot(hot(own == 12), got).astype(BF16)
    low = dot(hot(own == 13), got).astype(BF16)
    for k in range(TOP):
        at = row_ref[k : k + 1, :]
        mine = hot(iota((EXPERTS, TOK), 0) == lax.shift_right_logical(at, 5))
        score = dot_first(high, mine) + dot_first(low, mine)
        column = (at & (BLOCK - 1)) + FEAT
        d_probs_ref[k : k + 1, :] = jnp.sum(jnp.where(lane == column, score, 0.0), axis=0, keepdims=True)


def struct(*shape, dtype):
    return jax.ShapeDtypeStruct(shape, dtype)


SAME_CORE = [[2 * j + core for j in range(CHIPS)] for core in range(2)]

LINES = [
    [[2 * (SIDE * y + x) for x in range(SIDE)] for y in range(SIDE)],
    [[2 * (SIDE * y + x) + 1 for y in range(SIDE)] for x in range(SIDE)],
    [[2 * (SIDE * y + x) for y in range(SIDE)] for x in range(SIDE)],
    [[2 * (SIDE * y + x) + 1 for x in range(SIDE)] for y in range(SIDE)],
]
OTHER_CORE = [(i, i ^ 1) for i in range(2 * CHIPS)]


def per_device(tokens, grad_out, probs, routes, gate_weight, up_weight, down_weight):
    packed, row_of = pl.pallas_call(
        pack_kernel,
        out_shape=(pltpu.VMEM((EXPERTS, BLOCK, 128), BF16), pltpu.VMEM((8, TOK), I32)),
        in_specs=[pl.BlockSpec(memory_space=pltpu.HBM)] * 4,
        scratch_shapes=[
            pltpu.VMEM((TOP, TOK), I32),
            pltpu.VMEM((TOP, TOK), BF16),
            pltpu.VMEM((TOK, FEAT), BF16),
            pltpu.VMEM((TOK, FEAT), BF16),
            pltpu.SemaphoreType.DMA((4,)),
        ],
        compiler_params=params(60),
        name="pack",
    )(routes.T, probs.T, tokens, grad_out)
    got = lax.all_to_all(packed, "expert", 0, 0, tiled=True)
    copies, prob_rows = pl.pallas_call(
        spread_kernel,
        out_shape=(struct(SIDE, FEAT, 640, dtype=BF16), struct(8, WIDE, dtype=F32)),
        compiler_params=params(16),
        name="spread",
    )(got)
    line = lax.all_to_all(copies, "tensor", 0, 0, tiled=True, axis_index_groups=LINES[0] + LINES[1])
    lines = pl.pallas_call(
        relay_kernel,
        out_shape=struct(SIDE, SIDE, FEAT, 640, dtype=BF16),
        compiler_params=params(16),
        name="relay",
    )(line)
    own = lax.all_to_all(lines, "tensor", 0, 0, tiled=True, axis_index_groups=LINES[2] + LINES[3])
    other = lax.ppermute(own, "tensor", OTHER_CORE)
    rows, gate_t, up_t, far, near_pre, picks = pl.pallas_call(
        turn_kernel,
        out_shape=(
            struct(CHIPS, 2, FEAT, 640, dtype=BF16),
            struct(2, CHIPS, FEAT, HID, dtype=BF16),
            struct(2, CHIPS, FEAT, HID, dtype=BF16),
            struct(3, HID, D // 2, dtype=BF16),
            struct(3, HID, WIDE, dtype=F32),
            struct(4, TOK, EXPERTS * BACK, dtype=BF16),
        ),
        scratch_shapes=[pltpu.VMEM((3, HID, D // 2), BF16)],
        compiler_params=params(24),
        cost_estimate=cost(8e9),
        name="turn",
    )(own, gate_weight, up_weight, down_weight, row_of)
    rows, send, score, hid = pl.pallas_call(
        middle_kernel,
        out_shape=(
            struct(CHIPS, 2, FEAT, 640, dtype=BF16),
            struct(CHIPS, 256, 128, dtype=BF16),
            struct(16, 128, dtype=F32),
            struct(3, HID, WIDE, dtype=BF16),
        ),
        input_output_aliases={0: 0},
        compiler_params=params(24),
        cost_estimate=cost(4e9),
        name="middle",
    )(rows, other, far, near_pre, prob_rows, gate_t, up_t)
    partner = lax.ppermute(send, "tensor", OTHER_CORE)
    keep, d_down = pl.pallas_call(
        rest_kernel,
        out_shape=(struct(CHIPS, 240, 128, dtype=F32), struct(1, HID, D, dtype=BF16)),
        compiler_params=params(20),
        cost_estimate=cost(4e9),
        name="rest",
    )(rows, hid, gate_t, up_t)
    joined = pl.pallas_call(
        join_kernel,
        out_shape=struct(CHIPS, 256, 128, dtype=BF16),
        compiler_params=params(16),
        name="join",
    )(keep, score, partner)
    shares = lax.all_to_all(joined, "tensor", 0, 0, tiled=True, axis_index_groups=SAME_CORE)
    folded = pl.pallas_call(
        fold_kernel,
        out_shape=struct(EXPERTS, BACK, 128, dtype=BF16),
        compiler_params=params(16),
        name="fold",
    )(shares, jnp.asarray(fold_table()))
    back = lax.all_to_all(folded, "expert", 0, 0, tiled=True)
    d_tokens, d_probs = pl.pallas_call(
        combine_kernel,
        out_shape=(struct(TOK, FEAT, dtype=BF16), struct(TOP, TOK, dtype=F32)),
        compiler_params=params(16),
        name="combine",
    )(back, row_of, picks)
    return d_tokens, d_probs.T, d_down


def solution(mesh):
    return jax.shard_map(
        per_device,
        mesh=mesh,
        in_specs=(
            P("expert", "tensor"),
            P("expert", "tensor"),
            P("expert", None),
            P("expert", None),
            P("expert", "tensor", None),
            P("expert", "tensor", None),
            P("expert", "tensor", None),
        ),
        out_specs=(P("expert", "tensor"), P("expert", None), P("expert", "tensor", None)),
        check_vma=False,
    )
```

```python
import jax
import jax.numpy as jnp
import ml_dtypes
import numpy as np
from jax import lax
from jax.experimental import pallas as pl
from jax.experimental.pallas import tpu as pltpu
from jax.sharding import PartitionSpec as P

F32 = jnp.float32
BF16 = jnp.bfloat16
I32 = jnp.int32

EXPERTS = 16
CHIPS = 16
SIDE = 4
CAP = 20
SLOTS = EXPERTS * CAP
WIDE = 384
TOK = 64
TOP = 4
FEAT = 96
HID = 168
D = 3072
BLOCK = 32
BACK = 16


def iota(shape, dim):
    return lax.broadcasted_iota(I32, shape, dim)


def flag(condition):
    return jnp.where(condition, 1.0, 0.0).astype(F32)


def hot(condition):
    return flag(condition).astype(BF16)


def dot(a, b):
    return jnp.dot(a, b, preferred_element_type=F32)


def dot_first(a, b):
    return lax.dot_general(a, b, (((0,), (0,)), ((), ())), preferred_element_type=F32)


def dot_last(a, b):
    return lax.dot_general(a, b, (((1,), (1,)), ((), ())), preferred_element_type=F32)


def expert_of(slot):
    return lax.shift_right_logical(slot * 3277, 16)


def params(mib, **kw):
    return pltpu.CompilerParams(vmem_limit_bytes=mib * 1024 * 1024, **kw)


def cost(flops):
    return pl.CostEstimate(flops=int(flops), bytes_accessed=4 << 20, transcendentals=0)


def pack_kernel(routes_hbm, probs_hbm, x_hbm, dy_hbm, out_ref, row_ref, routes_ref, probs_ref, x_ref, dy_ref, sems):
    pairs = ((routes_hbm, routes_ref), (probs_hbm, probs_ref), (x_hbm, x_ref), (dy_hbm, dy_ref))
    loads = [pltpu.make_async_copy(src, dst, sems.at[i]) for i, (src, dst) in enumerate(pairs)]
    for load in loads:
        load.start()
    for load in loads:
        load.wait()
    routes = routes_ref[...]
    probs = probs_ref[...].astype(F32)
    experts = iota((EXPERTS, TOK), 0)
    hits = [routes[k : k + 1, :] == experts for k in range(TOP)]
    member = sum(flag(h) for h in hits)
    weight = sum(jnp.where(hits[k], probs[k : k + 1, :], 0.0) for k in range(TOP))
    upper = hot(iota((TOK, TOK), 0) < iota((TOK, TOK), 1))
    count = dot(member.astype(BF16), upper)
    place = jnp.where(member > 0.5, count, -1.0)
    target = count + (experts * BLOCK).astype(F32)
    rows_of = [jnp.sum(jnp.where(hits[k], target, 0.0), axis=0, keepdims=True) for k in range(TOP)]
    kth = iota((8, TOK), 0)
    row_ref[...] = sum(jnp.where(kth == k, rows_of[k], 0.0) for k in range(TOP)).astype(I32)

    rows = EXPERTS * BLOCK
    expand = hot(lax.shift_right_logical(iota((rows, EXPERTS), 0), 5) == iota((rows, EXPERTS), 1))
    place_rows = dot(expand, place.astype(BF16))
    s_int = iota((rows, TOK), 0) & (BLOCK - 1)
    s = s_int.astype(F32)
    tail = (s_int >= CAP) & (s_int < 30)
    main = hot((place_rows == s) & (s_int < CAP))
    left = hot((place_rows == s - 20.0) & tail)
    right = hot((place_rows == s - 10.0) & tail)

    x = x_ref[...]
    dy = dy_ref[...]
    f = iota((FEAT, 128), 0)
    lane = iota((FEAT, 128), 1)
    b_main = dot(x, hot(lane == f)) + dot(dy, hot((lane == f + 96) & (f < 32)))
    b_left = dot(dy, hot((lane == f - 32) & (f >= 32)))
    b_right = dot(dy, hot((lane == f + 32) & (f >= 32)))

    lane_e = iota((EXPERTS, 128), 1)
    prob_block = jnp.zeros((EXPERTS, 128), F32)
    for j in range(CAP):
        column = jnp.sum(jnp.where(place == float(j), weight, 0.0), axis=1, keepdims=True)
        prob_block = jnp.where(lane_e == j, column, prob_block)
    prob_block = prob_block.astype(BF16)
    at_30 = hot(iota((rows, EXPERTS), 0) == iota((rows, EXPERTS), 1) * BLOCK + 30)

    out = (
        dot(main, b_main.astype(BF16))
        + dot(left, b_left.astype(BF16))
        + dot(right, b_right.astype(BF16))
        + dot(at_30, prob_block)
    )
    out_ref[...] = out.astype(BF16).reshape(EXPERTS, BLOCK, 128)


def fold_table():
    n = np.arange(WIDE)
    r = np.arange(EXPERTS * BACK)[:, None]
    e, s = n // CAP, n % CAP
    masks = [(r == e * BACK + s) & (s < BACK)]
    masks += [(r == e * BACK + 3 * (s - BACK) + q) & (s >= BACK) for q in range(3)]
    masks += [r == e * BACK + 12, r == e * BACK + 13]
    return (np.stack(masks) & (n < SLOTS)).astype(ml_dtypes.bfloat16)


def spread_kernel(got_ref, out_ref, prob_ref):
    rows = EXPERTS * BLOCK
    got = got_ref[...].reshape(rows, 128)
    n = iota((1, WIDE), 1)
    e_x = expert_of(n)
    s_x = n - e_x * CAP
    to_x = jnp.where(n < SLOTS, e_x * BLOCK + s_x, -1)
    slot = jnp.where(n < 128, n + 192, n - 128)
    e_d = expert_of(slot)
    s_d = slot - e_d * CAP
    live = n >= 64
    to_d = jnp.where(live, e_d * BLOCK + s_d, -1)
    to_left = jnp.where(live & (s_d < 10), e_d * BLOCK + 20 + s_d, -1)
    to_right = jnp.where(live & (s_d >= 10), e_d * BLOCK + 10 + s_d, -1)
    r = iota((rows, WIDE), 0)
    got_t = got.T
    part_x = dot(got_t, hot(r == to_x))
    part_d = dot(got_t, hot(r == to_d))
    both = hot(r == to_left + to_right + 1)
    mixed = dot(got_t, both)
    part_l = jnp.where(s_d < 10, mixed, 0.0)
    part_r = jnp.where(s_d < 10, 0.0, mixed)
    x_t = part_x[0:FEAT]
    d_t = jnp.concatenate([part_d[96:128], part_l[0:64] + part_r[64:128]], axis=0)
    first = x_t[:, 0:256].astype(BF16)
    middle = (x_t[:, 256:384] + d_t[:, 0:128]).astype(BF16)
    last = d_t[:, 128:384].astype(BF16)
    for j in range(SIDE):
        out_ref[j, :, 0:256] = first
        out_ref[j, :, 256:384] = middle
        out_ref[j, :, 384:640] = last

    pick = hot(iota((EXPERTS, rows), 1) == iota((EXPERTS, rows), 0) * BLOCK + 30)
    per_expert = dot(pick, got).astype(BF16)
    wide = dot(per_expert, hot(iota((128, WIDE), 0) == s_x))
    probs = jnp.sum(jnp.where(iota((EXPERTS, WIDE), 0) == e_x, wide, 0.0), axis=0, keepdims=True)
    prob_ref[...] = jnp.broadcast_to(probs, (8, WIDE))


def score_rows(scores):
    row = iota((16, 128), 0)
    return (
        jnp.where(row == 0, scores[:, 0:128], 0.0)
        + jnp.where(row == 1, scores[:, 128:256], 0.0)
        + jnp.where(row == 2, scores[:, 256:384], 0.0)
    )


def split_rows(scores):
    high = scores.astype(BF16).astype(F32)
    low = (scores - high).astype(BF16).astype(F32)
    return (high + pltpu.roll(low, 3, 0)).astype(BF16)


def squeeze(piece):
    last = piece[:, 256:384]
    lane = iota((48, 128), 1)
    both = jnp.where(lane < 64, last[0:48], pltpu.roll(last[48:96], 64, 1))
    return piece[:, 0:128], piece[:, 128:256], both


def this_core():
    return lax.rem(lax.axis_index("tensor"), 2)


def relay_kernel(got_ref, out_ref):
    for j in range(SIDE):
        out_ref[j] = got_ref[...]


def chip_of(i, core):
    return jnp.where(core == 0, i, (i % SIDE) * SIDE + i // SIDE)


def pick_routes(row_ref, pick_ref):
    places = row_ref[...].astype(F32).T.astype(I32)
    r = iota((TOK, EXPERTS * BACK), 1)
    picks = [jnp.zeros(r.shape, F32)] * 4
    for k in range(TOP):
        at = places[:, k : k + 1]
        slot = at & (BLOCK - 1)
        base = lax.shift_right_logical(at, 5) * BACK
        first = jnp.where(slot < BACK, base + slot, -1)
        later = jnp.where(slot < BACK, -3, base + 3 * (slot - BACK))
        picks[0] = picks[0] + flag(r == first)
        for q in range(3):
            picks[1 + q] = picks[1 + q] + flag(r == later + q)
    for q in range(4):
        pick_ref[q] = picks[q].astype(BF16)


def turn_kernel(
    own_ref,
    gate_ref,
    up_ref,
    down_ref,
    row_ref,
    rows_ref,
    gate_t_ref,
    up_t_ref,
    far_ref,
    near_pre_ref,
    pick_ref,
    near_ref,
):
    core = this_core()
    first = core == 0
    for i in range(CHIPS):
        rows_ref[chip_of(i, core), core] = own_ref[i // SIDE, i % SIDE, :, 256:640]
    for w, weight_ref in enumerate((gate_ref, up_ref, down_ref)):
        weight = weight_ref[0]
        for q in range(4):
            even = [192 * (SIDE * q + p) for p in range(4)]
            odd = [192 * (SIDE * p + q) + 96 for p in range(4)]
            even = jnp.concatenate([weight[:, c : c + 96] for c in even], axis=1)
            odd = jnp.concatenate([weight[:, c : c + 96] for c in odd], axis=1)
            near = jnp.where(first, even, odd)
            far = jnp.where(first, odd, even)
            at = pl.ds(q * 384, 384)
            near_ref[w, :, at] = near
            far_ref[w, :, at] = far
            if w < 2:
                turned_ref = (gate_t_ref, up_t_ref)[w]
                turned_ref[0, pl.ds(q * 4, 4)] = far.T.reshape(4, FEAT, HID)
                turned_ref[1, pl.ds(q * 4, 4)] = near.T.reshape(4, FEAT, HID)
    rows = own_ref[...].reshape(D // 2, 640)
    near_pre_ref[0] = dot(near_ref[0], rows[:, 0:384])
    near_pre_ref[1] = dot(near_ref[1], rows[:, 0:384])
    near_pre_ref[2] = dot(near_ref[2], rows[:, 256:640])
    pick_routes(row_ref, pick_ref)


def input_grads(turned, gate_t_ref, up_t_ref, grad_gate, grad_up, out_ref):
    for i in range(0, CHIPS, 4):
        part = pl.ds(i, 4)
        sums = dot(gate_t_ref[turned, part].reshape(384, HID), grad_gate)
        sums = sums + dot(up_t_ref[turned, part].reshape(384, HID), grad_up)
        for j in range(4):
            a, b, c = squeeze(sums[96 * j : 96 * j + 96])
            out_ref[i + j, 0:96] = a.astype(out_ref.dtype)
            out_ref[i + j, 96:192] = b.astype(out_ref.dtype)
            out_ref[i + j, 192:240] = c.astype(out_ref.dtype)


def middle_kernel(
    other_ref, far_ref, near_pre_ref, prob_ref, gate_t_ref, up_t_ref, send_ref, score_ref, hid_ref
):
    rows = other_ref[...].reshape(D // 2, 640)
    x_t = rows[:, 0:384]
    dy_t = rows[:, 256:640]
    pre_gate = near_pre_ref[0] + dot(far_ref[0], x_t)
    pre_up = near_pre_ref[1] + dot(far_ref[1], x_t)
    raw = near_pre_ref[2] + dot(far_ref[2], dy_t)
    back = jnp.concatenate([raw[:, 128:384], pltpu.roll(raw[:, 0:128], 64, 1)], axis=1)
    live = iota((1, WIDE), 1) < SLOTS
    back = jnp.where(live, back, 0.0)
    probs = prob_ref[0:1, :]
    sig = jax.nn.sigmoid(pre_gate)
    silu = pre_gate * sig
    hidden = (silu * pre_up).astype(BF16).astype(F32)
    scores = score_rows(jnp.sum(hidden * back, axis=0, keepdims=True))
    scaled = jnp.where(live, probs * hidden, 0.0)
    back_p = probs * back
    grad_gate = jnp.where(live, back_p * pre_up * sig * (1.0 + pre_gate * (1.0 - sig)), 0.0).astype(BF16)
    grad_up = (back_p * silu).astype(BF16)
    input_grads(0, gate_t_ref, up_t_ref, grad_gate, grad_up, send_ref)
    parts = split_rows(scores)
    for j in range(CHIPS):
        send_ref[j, 240:256] = parts
    score_ref[...] = scores
    scaled = jnp.concatenate([pltpu.roll(scaled[:, 256:384], 64, 1), scaled[:, 0:256]], axis=1)
    hid_ref[0] = scaled.astype(BF16)
    hid_ref[1] = grad_gate
    hid_ref[2] = grad_up


def rest_kernel(rows_in_ref, other_ref, hid_ref, gate_t_ref, up_t_ref, keep_ref, d_down_ref, rows_ref):
    del rows_in_ref
    core = this_core()
    for i in range(CHIPS):
        rows_ref[chip_of(i, 1 - core), 1 - core] = other_ref[i // SIDE, i % SIDE, :, 256:640]
    d_down_ref[0] = dot_last(hid_ref[0], rows_ref[...].reshape(D, WIDE)).astype(BF16)
    input_grads(1, gate_t_ref, up_t_ref, hid_ref[1], hid_ref[2], keep_ref)


def join_kernel(keep_ref, score_ref, got_ref, out_ref):
    got = got_ref[0, 240:256].astype(F32)
    row = iota((16, 128), 0)
    total = score_ref[...] + got + pltpu.roll(got, 13, 0)
    parts = split_rows(jnp.where(row < 3, total, 0.0))
    core = this_core()
    for i in range(CHIPS):
        j = chip_of(i, core)
        out_ref[j, 0:240] = (keep_ref[i, 0:240] + got_ref[i, 0:240].astype(F32)).astype(BF16)
        out_ref[j, 240:256] = parts


def fold_kernel(got_ref, table_ref, out_ref):
    total = got_ref[0].astype(F32)
    for j in range(1, CHIPS):
        total = total + got_ref[j].astype(F32)
    both = total[192:240]
    lane = iota((48, 128), 1)
    last = jnp.concatenate(
        [jnp.where(lane < 64, both, 0.0), jnp.where(lane < 64, pltpu.roll(both, 64, 1), 0.0)], axis=0
    )
    grads = jnp.concatenate([total[0:96], total[96:192], last], axis=1)
    tail = total[240:256]
    score = tail + pltpu.roll(tail, 13, 0)
    wide = jnp.concatenate([score[0:1], score[1:2], score[2:3]], axis=1)
    high = wide.astype(BF16).astype(F32)
    low = wide - high
    n = iota((1, WIDE), 1)
    e = expert_of(n)
    slot = n - e * CAP
    upper = jnp.concatenate([grads, jnp.zeros((32, WIDE), F32)], axis=0).astype(BF16)
    out = dot_last(table_ref[0], upper)
    for q in range(3):
        part = jnp.concatenate([jnp.zeros((FEAT, WIDE), F32), grads[32 * q : 32 * q + 32]], axis=0).astype(BF16)
        out = out + dot_last(table_ref[1 + q], part)
    values = table_ref[4].astype(F32) * high + table_ref[5].astype(F32) * low
    out = out + dot_last(values.astype(BF16), hot(iota((128, WIDE), 0) == slot + FEAT))
    out_ref[...] = out.astype(BF16).reshape(EXPERTS, BACK, 128)


def combine_kernel(got_ref, row_ref, pick_ref, d_tokens_ref, d_probs_ref):
    rows = EXPERTS * BACK
    got = got_ref[...].reshape(rows, 128)
    total = dot(pick_ref[0], got)
    feature = iota((TOK, 128), 1)
    for q in range(3):
        part = pltpu.roll(dot(pick_ref[1 + q], got), 32 + 32 * q, 1)
        total = total + jnp.where(lax.shift_right_logical(feature, 5) == q, part, 0.0)
    d_tokens_ref[...] = total[:, 0:FEAT].astype(BF16)
    lane = iota((128, TOK), 0)
    own = iota((EXPERTS, rows), 1) - iota((EXPERTS, rows), 0) * BACK
    high = dot(hot(own == 12), got).astype(BF16)
    low = dot(hot(own == 13), got).astype(BF16)
    for k in range(TOP):
        at = row_ref[k : k + 1, :]
        mine = hot(iota((EXPERTS, TOK), 0) == lax.shift_right_logical(at, 5))
        score = dot_first(high, mine) + dot_first(low, mine)
        column = (at & (BLOCK - 1)) + FEAT
        d_probs_ref[k : k + 1, :] = jnp.sum(jnp.where(lane == column, score, 0.0), axis=0, keepdims=True)


def struct(*shape, dtype):
    return jax.ShapeDtypeStruct(shape, dtype)


SAME_CORE = [[2 * j + core for j in range(CHIPS)] for core in range(2)]

LINES = [
    [[2 * (SIDE * y + x) for x in range(SIDE)] for y in range(SIDE)],
    [[2 * (SIDE * y + x) + 1 for y in range(SIDE)] for x in range(SIDE)],
    [[2 * (SIDE * y + x) for y in range(SIDE)] for x in range(SIDE)],
    [[2 * (SIDE * y + x) + 1 for x in range(SIDE)] for y in range(SIDE)],
]
OTHER_CORE = [(i, i ^ 1) for i in range(2 * CHIPS)]


def per_device(tokens, grad_out, probs, routes, gate_weight, up_weight, down_weight):
    packed, row_of = pl.pallas_call(
        pack_kernel,
        out_shape=(pltpu.VMEM((EXPERTS, BLOCK, 128), BF16), pltpu.VMEM((8, TOK), I32)),
        in_specs=[pl.BlockSpec(memory_space=pltpu.HBM)] * 4,
        scratch_shapes=[
            pltpu.VMEM((TOP, TOK), I32),
            pltpu.VMEM((TOP, TOK), BF16),
            pltpu.VMEM((TOK, FEAT), BF16),
            pltpu.VMEM((TOK, FEAT), BF16),
            pltpu.SemaphoreType.DMA((4,)),
        ],
        compiler_params=params(60),
        name="pack",
    )(routes.T, probs.T, tokens, grad_out)
    got = lax.all_to_all(packed, "expert", 0, 0, tiled=True)
    copies, prob_rows = pl.pallas_call(
        spread_kernel,
        out_shape=(struct(SIDE, FEAT, 640, dtype=BF16), struct(8, WIDE, dtype=F32)),
        compiler_params=params(16),
        name="spread",
    )(got)
    line = lax.all_to_all(copies, "tensor", 0, 0, tiled=True, axis_index_groups=LINES[0] + LINES[1])
    lines = pl.pallas_call(
        relay_kernel,
        out_shape=struct(SIDE, SIDE, FEAT, 640, dtype=BF16),
        compiler_params=params(16),
        name="relay",
    )(line)
    own = lax.all_to_all(lines, "tensor", 0, 0, tiled=True, axis_index_groups=LINES[2] + LINES[3])
    other = lax.ppermute(own, "tensor", OTHER_CORE)
    rows, gate_t, up_t, far, near_pre, picks = pl.pallas_call(
        turn_kernel,
        out_shape=(
            struct(CHIPS, 2, FEAT, WIDE, dtype=BF16),
            struct(2, CHIPS, FEAT, HID, dtype=BF16),
            struct(2, CHIPS, FEAT, HID, dtype=BF16),
            struct(3, HID, D // 2, dtype=BF16),
            struct(3, HID, WIDE, dtype=F32),
            struct(4, TOK, EXPERTS * BACK, dtype=BF16),
        ),
        scratch_shapes=[pltpu.VMEM((3, HID, D // 2), BF16)],
        compiler_params=params(24),
        cost_estimate=cost(8e9),
        name="turn",
    )(own, gate_weight, up_weight, down_weight, row_of)
    send, score, hid = pl.pallas_call(
        middle_kernel,
        out_shape=(
            struct(CHIPS, 256, 128, dtype=BF16),
            struct(16, 128, dtype=F32),
            struct(3, HID, WIDE, dtype=BF16),
        ),
        compiler_params=params(24),
        cost_estimate=cost(4e9),
        name="middle",
    )(other, far, near_pre, prob_rows, gate_t, up_t)
    partner = lax.ppermute(send, "tensor", OTHER_CORE)
    keep, d_down, _ = pl.pallas_call(
        rest_kernel,
        out_shape=(
            struct(CHIPS, 240, 128, dtype=F32),
            struct(1, HID, D, dtype=BF16),
            struct(CHIPS, 2, FEAT, WIDE, dtype=BF16),
        ),
        input_output_aliases={0: 2},
        compiler_params=params(20),
        cost_estimate=cost(4e9),
        name="rest",
    )(rows, other, hid, gate_t, up_t)
    joined = pl.pallas_call(
        join_kernel,
        out_shape=struct(CHIPS, 256, 128, dtype=BF16),
        compiler_params=params(16),
        name="join",
    )(keep, score, partner)
    shares = lax.all_to_all(joined, "tensor", 0, 0, tiled=True, axis_index_groups=SAME_CORE)
    folded = pl.pallas_call(
        fold_kernel,
        out_shape=struct(EXPERTS, BACK, 128, dtype=BF16),
        compiler_params=params(16),
        name="fold",
    )(shares, jnp.asarray(fold_table()))
    back = lax.all_to_all(folded, "expert", 0, 0, tiled=True)
    d_tokens, d_probs = pl.pallas_call(
        combine_kernel,
        out_shape=(struct(TOK, FEAT, dtype=BF16), struct(TOP, TOK, dtype=F32)),
        compiler_params=params(16),
        name="combine",
    )(back, row_of, picks)
    return d_tokens, d_probs.T, d_down


def solution(mesh):
    return jax.shard_map(
        per_device,
        mesh=mesh,
        in_specs=(
            P("expert", "tensor"),
            P("expert", "tensor"),
            P("expert", None),
            P("expert", None),
            P("expert", "tensor", None),
            P("expert", "tensor", None),
            P("expert", "tensor", None),
        ),
        out_specs=(P("expert", "tensor"), P("expert", None), P("expert", "tensor", None)),
        check_vma=False,
    )
```

```python
import jax
import jax.numpy as jnp
import ml_dtypes
import numpy as np
from jax import lax
from jax.experimental import pallas as pl
from jax.experimental.pallas import tpu as pltpu
from jax.sharding import PartitionSpec as P

F32 = jnp.float32
BF16 = jnp.bfloat16
I32 = jnp.int32

EXPERTS = 16
CHIPS = 16
SIDE = 4
CAP = 20
SLOTS = EXPERTS * CAP
WIDE = 384
TOK = 64
TOP = 4
FEAT = 96
HID = 168
D = 3072
BLOCK = 32
BACK = 16


def iota(shape, dim):
    return lax.broadcasted_iota(I32, shape, dim)


def flag(condition):
    return jnp.where(condition, 1.0, 0.0).astype(F32)


def hot(condition):
    return flag(condition).astype(BF16)


def dot(a, b):
    return jnp.dot(a, b, preferred_element_type=F32)


def dot_first(a, b):
    return lax.dot_general(a, b, (((0,), (0,)), ((), ())), preferred_element_type=F32)


def dot_last(a, b):
    return lax.dot_general(a, b, (((1,), (1,)), ((), ())), preferred_element_type=F32)


def expert_of(slot):
    return lax.shift_right_logical(slot * 3277, 16)


def params(mib, **kw):
    return pltpu.CompilerParams(vmem_limit_bytes=mib * 1024 * 1024, **kw)


def cost(flops):
    return pl.CostEstimate(flops=int(flops), bytes_accessed=4 << 20, transcendentals=0)


def pack_kernel(routes_hbm, probs_hbm, x_hbm, dy_hbm, out_ref, row_ref, routes_ref, probs_ref, x_ref, dy_ref, sems):
    pairs = ((routes_hbm, routes_ref), (probs_hbm, probs_ref), (x_hbm, x_ref), (dy_hbm, dy_ref))
    loads = [pltpu.make_async_copy(src, dst, sems.at[i]) for i, (src, dst) in enumerate(pairs)]
    for load in loads:
        load.start()
    for load in loads:
        load.wait()
    routes = routes_ref[...]
    probs = probs_ref[...].astype(F32)
    experts = iota((EXPERTS, TOK), 0)
    hits = [routes[k : k + 1, :] == experts for k in range(TOP)]
    member = sum(flag(h) for h in hits)
    weight = sum(jnp.where(hits[k], probs[k : k + 1, :], 0.0) for k in range(TOP))
    upper = hot(iota((TOK, TOK), 0) < iota((TOK, TOK), 1))
    count = dot(member.astype(BF16), upper)
    place = jnp.where(member > 0.5, count, -1.0)
    target = count + (experts * BLOCK).astype(F32)
    rows_of = [jnp.sum(jnp.where(hits[k], target, 0.0), axis=0, keepdims=True) for k in range(TOP)]
    kth = iota((8, TOK), 0)
    row_ref[...] = sum(jnp.where(kth == k, rows_of[k], 0.0) for k in range(TOP)).astype(I32)

    rows = EXPERTS * BLOCK
    expand = hot(lax.shift_right_logical(iota((rows, EXPERTS), 0), 5) == iota((rows, EXPERTS), 1))
    place_rows = dot(expand, place.astype(BF16))
    s_int = iota((rows, TOK), 0) & (BLOCK - 1)
    s = s_int.astype(F32)
    tail = (s_int >= CAP) & (s_int < 30)
    main = hot((place_rows == s) & (s_int < CAP))
    left = hot((place_rows == s - 20.0) & tail)
    right = hot((place_rows == s - 10.0) & tail)

    x = x_ref[...]
    dy = dy_ref[...]
    f = iota((FEAT, 128), 0)
    lane = iota((FEAT, 128), 1)
    b_main = dot(x, hot(lane == f)) + dot(dy, hot((lane == f + 96) & (f < 32)))
    b_left = dot(dy, hot((lane == f - 32) & (f >= 32)))
    b_right = dot(dy, hot((lane == f + 32) & (f >= 32)))

    lane_e = iota((EXPERTS, 128), 1)
    prob_block = jnp.zeros((EXPERTS, 128), F32)
    for j in range(CAP):
        column = jnp.sum(jnp.where(place == float(j), weight, 0.0), axis=1, keepdims=True)
        prob_block = jnp.where(lane_e == j, column, prob_block)
    prob_block = prob_block.astype(BF16)
    at_30 = hot(iota((rows, EXPERTS), 0) == iota((rows, EXPERTS), 1) * BLOCK + 30)

    out = (
        dot(main, b_main.astype(BF16))
        + dot(left, b_left.astype(BF16))
        + dot(right, b_right.astype(BF16))
        + dot(at_30, prob_block)
    )
    out_ref[...] = out.astype(BF16).reshape(EXPERTS, BLOCK, 128)


def fold_table():
    n = np.arange(WIDE)
    r = np.arange(EXPERTS * BACK)[:, None]
    e, s = n // CAP, n % CAP
    masks = [(r == e * BACK + s) & (s < BACK)]
    masks += [(r == e * BACK + 3 * (s - BACK) + q) & (s >= BACK) for q in range(3)]
    masks += [r == e * BACK + 12, r == e * BACK + 13]
    return (np.stack(masks) & (n < SLOTS)).astype(ml_dtypes.bfloat16)


def spread_kernel(got_ref, out_ref, prob_ref):
    rows = EXPERTS * BLOCK
    got = got_ref[...].reshape(rows, 128)
    n = iota((1, WIDE), 1)
    e_x = expert_of(n)
    s_x = n - e_x * CAP
    to_x = jnp.where(n < SLOTS, e_x * BLOCK + s_x, -1)
    slot = jnp.where(n < 128, n + 192, n - 128)
    e_d = expert_of(slot)
    s_d = slot - e_d * CAP
    live = n >= 64
    to_d = jnp.where(live, e_d * BLOCK + s_d, -1)
    to_left = jnp.where(live & (s_d < 10), e_d * BLOCK + 20 + s_d, -1)
    to_right = jnp.where(live & (s_d >= 10), e_d * BLOCK + 10 + s_d, -1)
    r = iota((rows, WIDE), 0)
    got_t = got.T
    part_x = dot(got_t, hot(r == to_x))
    part_d = dot(got_t, hot(r == to_d))
    both = hot(r == to_left + to_right + 1)
    mixed = dot(got_t, both)
    part_l = jnp.where(s_d < 10, mixed, 0.0)
    part_r = jnp.where(s_d < 10, 0.0, mixed)
    x_t = part_x[0:FEAT]
    d_t = jnp.concatenate([part_d[96:128], part_l[0:64] + part_r[64:128]], axis=0)
    first = x_t[:, 0:256].astype(BF16)
    middle = (x_t[:, 256:384] + d_t[:, 0:128]).astype(BF16)
    last = d_t[:, 128:384].astype(BF16)
    for j in range(SIDE):
        out_ref[j, :, 0:256] = first
        out_ref[j, :, 256:384] = middle
        out_ref[j, :, 384:640] = last

    pick = hot(iota((EXPERTS, rows), 1) == iota((EXPERTS, rows), 0) * BLOCK + 30)
    per_expert = dot(pick, got).astype(BF16)
    wide = dot(per_expert, hot(iota((128, WIDE), 0) == s_x))
    probs = jnp.sum(jnp.where(iota((EXPERTS, WIDE), 0) == e_x, wide, 0.0), axis=0, keepdims=True)
    prob_ref[...] = jnp.broadcast_to(probs, (8, WIDE))


def score_rows(scores):
    row = iota((16, 128), 0)
    return (
        jnp.where(row == 0, scores[:, 0:128], 0.0)
        + jnp.where(row == 1, scores[:, 128:256], 0.0)
        + jnp.where(row == 2, scores[:, 256:384], 0.0)
    )


def split_rows(scores):
    high = scores.astype(BF16).astype(F32)
    low = (scores - high).astype(BF16).astype(F32)
    return (high + pltpu.roll(low, 3, 0)).astype(BF16)


def squeeze(piece):
    last = piece[:, 256:384]
    lane = iota((48, 128), 1)
    both = jnp.where(lane < 64, last[0:48], pltpu.roll(last[48:96], 64, 1))
    return piece[:, 0:128], piece[:, 128:256], both


def this_core():
    return lax.rem(lax.axis_index("tensor"), 2)


def relay_kernel(got_ref, out_ref):
    for j in range(SIDE):
        out_ref[j] = got_ref[...]


def chip_of(i, core):
    return jnp.where(core == 0, i, (i % SIDE) * SIDE + i // SIDE)


def pick_routes(row_ref, pick_ref):
    places = row_ref[...].astype(F32).T.astype(I32)
    r = iota((TOK, EXPERTS * BACK), 1)
    picks = [jnp.zeros(r.shape, F32)] * 4
    for k in range(TOP):
        at = places[:, k : k + 1]
        slot = at & (BLOCK - 1)
        base = lax.shift_right_logical(at, 5) * BACK
        first = jnp.where(slot < BACK, base + slot, -1)
        later = jnp.where(slot < BACK, -3, base + 3 * (slot - BACK))
        picks[0] = picks[0] + flag(r == first)
        for q in range(3):
            picks[1 + q] = picks[1 + q] + flag(r == later + q)
    for q in range(4):
        pick_ref[q] = picks[q].astype(BF16)


def turn_kernel(
    own_ref,
    gate_ref,
    up_ref,
    down_ref,
    row_ref,
    rows_ref,
    gate_t_ref,
    up_t_ref,
    far_ref,
    near_pre_ref,
    pick_ref,
    near_ref,
):
    core = this_core()
    first = core == 0
    for i in range(CHIPS):
        rows_ref[chip_of(i, core), core] = own_ref[i // SIDE, i % SIDE, :, 256:640]
    for w, weight_ref in enumerate((gate_ref, up_ref, down_ref)):
        weight = weight_ref[0]
        for q in range(4):
            even = [192 * (SIDE * q + p) for p in range(4)]
            odd = [192 * (SIDE * p + q) + 96 for p in range(4)]
            even = jnp.concatenate([weight[:, c : c + 96] for c in even], axis=1)
            odd = jnp.concatenate([weight[:, c : c + 96] for c in odd], axis=1)
            near = jnp.where(first, even, odd)
            far = jnp.where(first, odd, even)
            at = pl.ds(q * 384, 384)
            near_ref[w, :, at] = near
            far_ref[w, :, at] = far
            if w < 2:
                turned_ref = (gate_t_ref, up_t_ref)[w]
                turned_ref[0, pl.ds(q * 4, 4)] = far.T.reshape(4, FEAT, HID)
                turned_ref[1, pl.ds(q * 4, 4)] = near.T.reshape(4, FEAT, HID)
    rows = own_ref[...].reshape(D // 2, 640)
    near_pre_ref[0] = dot(near_ref[0], rows[:, 0:384])
    near_pre_ref[1] = dot(near_ref[1], rows[:, 0:384])
    near_pre_ref[2] = dot(near_ref[2], rows[:, 256:640])
    pick_routes(row_ref, pick_ref)


def input_grads(turned, gate_t_ref, up_t_ref, grad_gate, grad_up, out_ref):
    for i in range(0, CHIPS, 4):
        part = pl.ds(i, 4)
        sums = dot(gate_t_ref[turned, part].reshape(384, HID), grad_gate)
        sums = sums + dot(up_t_ref[turned, part].reshape(384, HID), grad_up)
        for j in range(4):
            a, b, c = squeeze(sums[96 * j : 96 * j + 96])
            out_ref[i + j, 0:96] = a.astype(out_ref.dtype)
            out_ref[i + j, 96:192] = b.astype(out_ref.dtype)
            out_ref[i + j, 192:240] = c.astype(out_ref.dtype)


def middle_kernel(
    other_ref, far_ref, near_pre_ref, prob_ref, gate_t_ref, up_t_ref, send_ref, score_ref, hid_ref
):
    rows = other_ref[...].reshape(D // 2, 640)
    x_t = rows[:, 0:384]
    dy_t = rows[:, 256:640]
    pre_gate = near_pre_ref[0] + dot(far_ref[0], x_t)
    pre_up = near_pre_ref[1] + dot(far_ref[1], x_t)
    raw = near_pre_ref[2] + dot(far_ref[2], dy_t)
    back = jnp.concatenate([raw[:, 128:384], pltpu.roll(raw[:, 0:128], 64, 1)], axis=1)
    live = iota((1, WIDE), 1) < SLOTS
    back = jnp.where(live, back, 0.0)
    probs = prob_ref[0:1, :]
    sig = jax.nn.sigmoid(pre_gate)
    silu = pre_gate * sig
    hidden = (silu * pre_up).astype(BF16).astype(F32)
    scores = score_rows(jnp.sum(hidden * back, axis=0, keepdims=True))
    back_p = probs * back
    grad_gate = jnp.where(live, back_p * pre_up * sig * (1.0 + pre_gate * (1.0 - sig)), 0.0).astype(BF16)
    grad_up = (back_p * silu).astype(BF16)
    input_grads(0, gate_t_ref, up_t_ref, grad_gate, grad_up, send_ref)
    parts = split_rows(scores)
    for j in range(CHIPS):
        send_ref[j, 240:256] = parts
    score_ref[...] = scores
    hid_ref[0] = hidden.astype(BF16)
    hid_ref[1] = grad_gate
    hid_ref[2] = grad_up


def rest_kernel(
    rows_in_ref, other_ref, hid_ref, prob_ref, gate_t_ref, up_t_ref, keep_ref, d_down_ref, rows_ref
):
    del rows_in_ref
    core = this_core()
    for i in range(CHIPS):
        rows_ref[chip_of(i, 1 - core), 1 - core] = other_ref[i // SIDE, i % SIDE, :, 256:640]
    live = iota((1, WIDE), 1) < SLOTS
    scaled = jnp.where(live, prob_ref[0:1, :] * hid_ref[0].astype(F32), 0.0)
    scaled = jnp.concatenate([pltpu.roll(scaled[:, 256:384], 64, 1), scaled[:, 0:256]], axis=1).astype(BF16)
    d_down_ref[0] = dot_last(scaled, rows_ref[...].reshape(D, WIDE)).astype(BF16)
    input_grads(1, gate_t_ref, up_t_ref, hid_ref[1], hid_ref[2], keep_ref)


def join_kernel(keep_ref, score_ref, got_ref, out_ref):
    got = got_ref[0, 240:256].astype(F32)
    row = iota((16, 128), 0)
    total = score_ref[...] + got + pltpu.roll(got, 13, 0)
    parts = split_rows(jnp.where(row < 3, total, 0.0))
    core = this_core()
    for i in range(CHIPS):
        j = chip_of(i, core)
        out_ref[j, 0:240] = (keep_ref[i, 0:240] + got_ref[i, 0:240].astype(F32)).astype(BF16)
        out_ref[j, 240:256] = parts


def fold_kernel(got_ref, table_ref, out_ref):
    total = got_ref[0].astype(F32)
    for j in range(1, CHIPS):
        total = total + got_ref[j].astype(F32)
    both = total[192:240]
    lane = iota((48, 128), 1)
    last = jnp.concatenate(
        [jnp.where(lane < 64, both, 0.0), jnp.where(lane < 64, pltpu.roll(both, 64, 1), 0.0)], axis=0
    )
    grads = jnp.concatenate([total[0:96], total[96:192], last], axis=1)
    tail = total[240:256]
    score = tail + pltpu.roll(tail, 13, 0)
    wide = jnp.concatenate([score[0:1], score[1:2], score[2:3]], axis=1)
    high = wide.astype(BF16).astype(F32)
    low = wide - high
    n = iota((1, WIDE), 1)
    e = expert_of(n)
    slot = n - e * CAP
    upper = jnp.concatenate([grads, jnp.zeros((32, WIDE), F32)], axis=0).astype(BF16)
    out = dot_last(table_ref[0], upper)
    for q in range(3):
        part = jnp.concatenate([jnp.zeros((FEAT, WIDE), F32), grads[32 * q : 32 * q + 32]], axis=0).astype(BF16)
        out = out + dot_last(table_ref[1 + q], part)
    values = table_ref[4].astype(F32) * high + table_ref[5].astype(F32) * low
    out = out + dot_last(values.astype(BF16), hot(iota((128, WIDE), 0) == slot + FEAT))
    out_ref[...] = out.astype(BF16).reshape(EXPERTS, BACK, 128)


def combine_kernel(got_ref, row_ref, pick_ref, d_tokens_ref, d_probs_ref):
    rows = EXPERTS * BACK
    got = got_ref[...].reshape(rows, 128)
    total = dot(pick_ref[0], got)
    feature = iota((TOK, 128), 1)
    for q in range(3):
        part = pltpu.roll(dot(pick_ref[1 + q], got), 32 + 32 * q, 1)
        total = total + jnp.where(lax.shift_right_logical(feature, 5) == q, part, 0.0)
    d_tokens_ref[...] = total[:, 0:FEAT].astype(BF16)
    lane = iota((128, TOK), 0)
    own = iota((EXPERTS, rows), 1) - iota((EXPERTS, rows), 0) * BACK
    high = dot(hot(own == 12), got).astype(BF16)
    low = dot(hot(own == 13), got).astype(BF16)
    for k in range(TOP):
        at = row_ref[k : k + 1, :]
        mine = hot(iota((EXPERTS, TOK), 0) == lax.shift_right_logical(at, 5))
        score = dot_first(high, mine) + dot_first(low, mine)
        column = (at & (BLOCK - 1)) + FEAT
        d_probs_ref[k : k + 1, :] = jnp.sum(jnp.where(lane == column, score, 0.0), axis=0, keepdims=True)


def struct(*shape, dtype):
    return jax.ShapeDtypeStruct(shape, dtype)


SAME_CORE = [[2 * j + core for j in range(CHIPS)] for core in range(2)]

LINES = [
    [[2 * (SIDE * y + x) for x in range(SIDE)] for y in range(SIDE)],
    [[2 * (SIDE * y + x) + 1 for y in range(SIDE)] for x in range(SIDE)],
    [[2 * (SIDE * y + x) for y in range(SIDE)] for x in range(SIDE)],
    [[2 * (SIDE * y + x) + 1 for x in range(SIDE)] for y in range(SIDE)],
]
OTHER_CORE = [(i, i ^ 1) for i in range(2 * CHIPS)]


def per_device(tokens, grad_out, probs, routes, gate_weight, up_weight, down_weight):
    packed, row_of = pl.pallas_call(
        pack_kernel,
        out_shape=(pltpu.VMEM((EXPERTS, BLOCK, 128), BF16), pltpu.VMEM((8, TOK), I32)),
        in_specs=[pl.BlockSpec(memory_space=pltpu.HBM)] * 4,
        scratch_shapes=[
            pltpu.VMEM((TOP, TOK), I32),
            pltpu.VMEM((TOP, TOK), BF16),
            pltpu.VMEM((TOK, FEAT), BF16),
            pltpu.VMEM((TOK, FEAT), BF16),
            pltpu.SemaphoreType.DMA((4,)),
        ],
        compiler_params=params(60),
        name="pack",
    )(routes.T, probs.T, tokens, grad_out)
    got = lax.all_to_all(packed, "expert", 0, 0, tiled=True)
    copies, prob_rows = pl.pallas_call(
        spread_kernel,
        out_shape=(struct(SIDE, FEAT, 640, dtype=BF16), struct(8, WIDE, dtype=F32)),
        compiler_params=params(16),
        name="spread",
    )(got)
    line = lax.all_to_all(copies, "tensor", 0, 0, tiled=True, axis_index_groups=LINES[0] + LINES[1])
    lines = pl.pallas_call(
        relay_kernel,
        out_shape=struct(SIDE, SIDE, FEAT, 640, dtype=BF16),
        compiler_params=params(16),
        name="relay",
    )(line)
    own = lax.all_to_all(lines, "tensor", 0, 0, tiled=True, axis_index_groups=LINES[2] + LINES[3])
    other = lax.ppermute(own, "tensor", OTHER_CORE)
    rows, gate_t, up_t, far, near_pre, picks = pl.pallas_call(
        turn_kernel,
        out_shape=(
            struct(CHIPS, 2, FEAT, WIDE, dtype=BF16),
            struct(2, CHIPS, FEAT, HID, dtype=BF16),
            struct(2, CHIPS, FEAT, HID, dtype=BF16),
            struct(3, HID, D // 2, dtype=BF16),
            struct(3, HID, WIDE, dtype=F32),
            struct(4, TOK, EXPERTS * BACK, dtype=BF16),
        ),
        scratch_shapes=[pltpu.VMEM((3, HID, D // 2), BF16)],
        compiler_params=params(24),
        cost_estimate=cost(8e9),
        name="turn",
    )(own, gate_weight, up_weight, down_weight, row_of)
    send, score, hid = pl.pallas_call(
        middle_kernel,
        out_shape=(
            struct(CHIPS, 256, 128, dtype=BF16),
            struct(16, 128, dtype=F32),
            struct(3, HID, WIDE, dtype=BF16),
        ),
        compiler_params=params(24),
        cost_estimate=cost(4e9),
        name="middle",
    )(other, far, near_pre, prob_rows, gate_t, up_t)
    partner = lax.ppermute(send, "tensor", OTHER_CORE)
    keep, d_down, _ = pl.pallas_call(
        rest_kernel,
        out_shape=(
            struct(CHIPS, 240, 128, dtype=F32),
            struct(1, HID, D, dtype=BF16),
            struct(CHIPS, 2, FEAT, WIDE, dtype=BF16),
        ),
        input_output_aliases={0: 2},
        compiler_params=params(20),
        cost_estimate=cost(4e9),
        name="rest",
    )(rows, other, hid, prob_rows, gate_t, up_t)
    joined = pl.pallas_call(
        join_kernel,
        out_shape=struct(CHIPS, 256, 128, dtype=BF16),
        compiler_params=params(16),
        name="join",
    )(keep, score, partner)
    shares = lax.all_to_all(joined, "tensor", 0, 0, tiled=True, axis_index_groups=SAME_CORE)
    folded = pl.pallas_call(
        fold_kernel,
        out_shape=struct(EXPERTS, BACK, 128, dtype=BF16),
        compiler_params=params(16),
        name="fold",
    )(shares, jnp.asarray(fold_table()))
    back = lax.all_to_all(folded, "expert", 0, 0, tiled=True)
    d_tokens, d_probs = pl.pallas_call(
        combine_kernel,
        out_shape=(struct(TOK, FEAT, dtype=BF16), struct(TOP, TOK, dtype=F32)),
        compiler_params=params(16),
        name="combine",
    )(back, row_of, picks)
    return d_tokens, d_probs.T, d_down


def solution(mesh):
    return jax.shard_map(
        per_device,
        mesh=mesh,
        in_specs=(
            P("expert", "tensor"),
            P("expert", "tensor"),
            P("expert", None),
            P("expert", None),
            P("expert", "tensor", None),
            P("expert", "tensor", None),
            P("expert", "tensor", None),
        ),
        out_specs=(P("expert", "tensor"), P("expert", None), P("expert", "tensor", None)),
        check_vma=False,
    )
```
